128 devices in a mesh: kv: 32 (over x, z, core), head: 4 (over y).
Axes of the slice: x: 4, y: 4, z: 4, core: 2. Of those that a mesh axis runs over, the one named last changes fastest.
Arguments:
- query_heads: bfloat16 [16, 3, 128, 192], P(None, None, ('kv', 'head')), may hold values from -9 to 9
- key_up: bfloat16 [128, 128, 512], P(('kv', 'head')), may hold values from -0.5 to 0.5
- value_up: bfloat16 [128, 512, 128], P(('kv', 'head')), may hold values from -4 to 4
- output_weight: bfloat16 [16384, 7168], P(('kv', 'head')), may hold values from -0.046875 to 0.046875
- latent_cache: bfloat16 [16, 32768, 576], P(None, 'kv'), may hold values from -400 to 400
- lengths: int32 [16], replicated, may hold values from 32 to 32768, as said below
- positions: int32 [16], replicated, may hold values from 0 to 4095
Outputs:
- attended: bfloat16 [16, 3, 7168], P(None, None, ('kv', 'head'))
The draws below stay inside these ranges and needn't reach their ends.
Inputs may be any that keep to these rules, and one draw needn't show every extreme that they name: `lengths`: each rollout holds at least 32 filled positions; some rollout holds exactly 32768.
All inputs are finite; a program needn't handle non-finite values.
Results may differ from the reference program's by a relative error of at most 0.022.
Values may be sent and summed in bfloat16 or wider, within the bound.
A program may use at most 256 MiB of HBM per device.

```python
import jax
import jax.numpy as jnp
from jax import lax

H = 128
DN = 128
DR = 64
DC = 512
DV = 128
D = 7168
B = 16
S = 3
CACHE = 32768


def shared_draws(key):
    place_key = jax.random.fold_in(key, 101)
    query_key = jax.random.fold_in(key, 102)
    places = jax.random.randint(place_key, (B,), 0, 4096).astype(jnp.int32)
    raw = jax.random.truncated_normal(query_key, -4.5, 4.5, (B, S, H, DN + DR), jnp.float32)
    widths = jnp.concatenate([jnp.ones((DN,), jnp.float32), 2.0 * jnp.ones((DR,), jnp.float32)])
    queries = (raw * widths).astype(jnp.bfloat16)
    return (queries, places)


def draw_fill(key):
    key = jax.random.fold_in(key, 9)
    first_key, second_key = jax.random.split(key)
    filled = jax.random.randint(first_key, (B,), 32, CACHE + 1)
    chosen = jax.random.randint(second_key, (), 0, B)
    filled = jnp.where(jnp.arange(B) == chosen, CACHE, filled)
    return filled.astype(jnp.int32)


def draw_query_heads(key, part):
    queries, places = shared_draws(key)
    return queries


def draw_positions(key, part):
    queries, places = shared_draws(key)
    return places


def draw_lengths(key, part):
    return draw_fill(key)


def draw_latent_cache(key, part):
    key = jax.random.fold_in(key, 5)
    base = jax.random.truncated_normal(key, -4.5, 4.5, (B, CACHE, DC + DR), jnp.float32)
    return base.astype(jnp.bfloat16)


def block_levels(stream_key, shape, pieces, least, largest):
    level = 1.0
    for position, parts in pieces:
        heights = jax.random.uniform(jax.random.fold_in(jax.random.fold_in(stream_key, 6), position), (parts,), jnp.float32, least / len(pieces), largest / len(pieces))
        level = level * jnp.repeat(jnp.exp(heights), shape[position] // parts).reshape((-1,) + (1,) * (len(shape) - 1 - position))
    return level


def normal_values(stream_key, extent, deviation, bound, pieces=(), kind=jnp.bfloat16):
    values = deviation * jax.random.normal(stream_key, extent, jnp.float32)
    if pieces:
        values = values * block_levels(stream_key, extent, pieces, -0.22, 0.18)
    return jnp.clip(values, -bound, bound).astype(kind)


def setup_inputs(seed: int = 0) -> dict:
    key_of = jax.random.split(jax.random.key(seed), 8)
    return {
        "query_heads": draw_query_heads(jax.random.fold_in(key_of[7], 71), 0),
        "key_up": normal_values(key_of[1], (H, DN, DC), DN ** -0.5, 0.5, ((0, 128),)),
        "value_up": normal_values(key_of[2], (H, DC, DV), 2 ** -0.5, 4.0, ((0, 128),)),
        "output_weight": normal_values(key_of[3], (H * DV, D), (H * DV) ** -0.5, 0.046875, ((0, 128),)),
        "latent_cache": draw_latent_cache(jax.random.fold_in(key_of[7], 71), 0),
        "lengths": draw_lengths(jax.random.fold_in(key_of[7], 71), 0),
        "positions": draw_positions(jax.random.fold_in(key_of[7], 71), 0),
    }


def rotate_pairs(vectors, places):
    half_dim = vectors.shape[-1] // 2
    frequency = 10000.0 ** (-jnp.arange(half_dim).astype(vectors.dtype) / half_dim)
    angles = places.astype(vectors.dtype)[..., None] * frequency
    first_half = vectors[..., :half_dim]
    second_half = vectors[..., half_dim:]
    return jnp.concatenate([first_half * jnp.cos(angles) - second_half * jnp.sin(angles), second_half * jnp.cos(angles) + first_half * jnp.sin(angles)], axis=-1)

def reference(query_heads, key_up, value_up, output_weight, latent_cache, lengths, positions):
    query_float = query_heads.astype(jnp.float32)
    query_latent = jnp.einsum('bshn,hnc->bshc', query_float[..., :DN], key_up.astype(jnp.float32))
    places = positions[:, None] + jnp.arange(S, dtype=jnp.int32)[None, :]
    query_rotary = rotate_pairs(query_float[..., DN:], places[:, :, None])
    query_all = jnp.concatenate([query_latent, query_rotary], axis=-1).astype(jnp.bfloat16)
    score_scale = 1.0 / jnp.sqrt(jnp.float32(DN + DR))

    def attend_rollout(rollout_item):
        query_block, cache_block, length_now = rollout_item
        cache_float = cache_block.astype(jnp.float32)
        scores = jnp.einsum('shd,jd->shj', query_block.astype(jnp.float32), cache_float) * score_scale
        slots = jnp.arange(CACHE, dtype=jnp.int32)
        last_visible = length_now - S + jnp.arange(S, dtype=jnp.int32)
        visible = slots[None, None, :] <= last_visible[:, None, None]
        scores = jnp.where(visible, scores, -1e+30)
        row_top = lax.optimization_barrier(jnp.max(scores, axis=-1, keepdims=True))
        probs = jnp.where(visible, jnp.exp(scores - row_top), 0.0)
        probs_low = lax.optimization_barrier(probs.astype(jnp.bfloat16))
        numerators = jnp.einsum('shj,jc->shc', probs_low.astype(jnp.float32), cache_float[:, :DC])
        totals = lax.optimization_barrier(jnp.sum(probs, axis=-1))
        return (numerators / totals[..., None]).astype(jnp.bfloat16)
    latent_out = lax.map(attend_rollout, (query_all, latent_cache, lengths))
    head_values = jnp.einsum('bshc,hcv->bshv', latent_out.astype(jnp.float32), value_up.astype(jnp.float32)).astype(jnp.bfloat16)
    flat_values = head_values.reshape(B * S, H * DV)
    attended = jnp.dot(flat_values, output_weight, preferred_element_type=jnp.float32)
    return attended.reshape(B, S, D).astype(jnp.bfloat16)
```

```python
import jax
import jax.numpy as jnp
from jax import lax
from jax.sharding import PartitionSpec as P

DN = 128
DR = 64
DC = 512


def rotate_pairs(vectors, places):
    half_dim = vectors.shape[-1] // 2
    frequency = 10000.0 ** (-jnp.arange(half_dim).astype(vectors.dtype) / half_dim)
    angles = places.astype(vectors.dtype)[..., None] * frequency
    first_half = vectors[..., :half_dim]
    second_half = vectors[..., half_dim:]
    return jnp.concatenate(
        [
            first_half * jnp.cos(angles) - second_half * jnp.sin(angles),
            second_half * jnp.cos(angles) + first_half * jnp.sin(angles),
        ],
        axis=-1,
    )


def body(query_heads, key_up, value_up, output_weight, latent_cache, lengths, positions):
    rollouts = query_heads.shape[0]
    new_tokens = query_heads.shape[1]
    heads_mine = query_heads.shape[2]
    model_width = output_weight.shape[1]
    value_width = value_up.shape[2]
    query_latent = jnp.einsum(
        "bshn,hnc->bshc", query_heads[..., :DN], key_up, preferred_element_type=jnp.float32
    )
    places = positions[:, None] + jnp.arange(new_tokens, dtype=jnp.int32)[None, :]
    query_rotary = rotate_pairs(query_heads[..., DN:].astype(jnp.float32), places[:, :, None])
    query_mine = jnp.concatenate([query_latent, query_rotary], axis=-1).astype(jnp.bfloat16)
    query_group = lax.all_gather(query_mine, "kv", axis=2, tiled=True)
    shard_rows = latent_cache.shape[1]
    shard_index = lax.axis_index("kv")
    score_scale = 1.0 / jnp.sqrt(jnp.float32(DN + DR))
    scores = (
        jnp.einsum("bsgd,bjd->bsgj", query_group, latent_cache, preferred_element_type=jnp.float32)
        * score_scale
    )
    slots = shard_index * shard_rows + jnp.arange(shard_rows, dtype=jnp.int32)
    last_visible = lengths[:, None] - new_tokens + jnp.arange(new_tokens, dtype=jnp.int32)[None, :]
    visible = slots[None, None, None, :] <= last_visible[:, :, None, None]
    scores = jnp.where(visible, scores, -1e30)
    top = lax.pmax(jnp.max(scores, axis=-1), "kv")
    weights = jnp.where(visible, jnp.exp(scores - top[..., None]), 0.0)
    totals = jnp.sum(weights, axis=-1)
    numerators = jnp.einsum(
        "bsgj,bjc->gbsc",
        weights.astype(jnp.bfloat16),
        latent_cache[..., :DC],
        preferred_element_type=jnp.float32,
    )
    mine_numer = lax.psum_scatter(numerators, "kv", scatter_dimension=0, tiled=True)
    joint_total = lax.psum(totals, "kv")
    head_start = shard_index * heads_mine
    mine_total = lax.dynamic_slice_in_dim(joint_total, head_start, heads_mine, 2)
    mine_numer = jnp.transpose(mine_numer, (1, 2, 0, 3))
    latent_out = (mine_numer / mine_total[..., None]).astype(jnp.bfloat16)
    head_values = jnp.einsum(
        "bshc,hcv->bshv", latent_out, value_up, preferred_element_type=jnp.float32
    ).astype(jnp.bfloat16)
    flat_values = head_values.reshape(rollouts * new_tokens, heads_mine * value_width)
    head_term = jnp.dot(flat_values, output_weight, preferred_element_type=jnp.float32)
    head_term = head_term.reshape(rollouts, new_tokens, model_width)
    attended = lax.psum_scatter(head_term, ("kv", "head"), scatter_dimension=2, tiled=True)
    return attended.astype(jnp.bfloat16)


def solution(mesh):
    in_specs = (
        P(None, None, ("kv", "head"), None),
        P(("kv", "head"), None, None),
        P(("kv", "head"), None, None),
        P(("kv", "head"), None),
        P(None, "kv", None),
        P(),
        P(),
    )
    out_specs = P(None, None, ("kv", "head"))
    return jax.shard_map(body, mesh=mesh, in_specs=in_specs, out_specs=out_specs, check_vma=False)
```

```python
import functools

import jax
import jax.numpy as jnp
import numpy as np
from jax import lax
from jax.experimental import pallas as pl
from jax.experimental.pallas import tpu as pltpu
from jax.sharding import PartitionSpec as P

MESH = pl.DeviceIdType.MESH
BF = jnp.bfloat16
F32 = jnp.float32

DN = 128
DR = 64
DC = 512
B = 16
S = 3
ROWS = B * S
CHUNKS = ROWS // 16
RANK = DC + DR
WIDE = 640
SHARD = 1024
FEAT = 56
MASKED = -(2.0**100)
FACTOR = float(np.log2(np.e) / np.sqrt(DN + DR))

dot = functools.partial(lax.dot_general, preferred_element_type=F32)
NN = (((1,), (0,)), ((), ()))
NT = (((1,), (1,)), ((), ()))


def split3(value):
    high = value.astype(BF).astype(F32)
    rest = value - high
    middle = rest.astype(BF).astype(F32)
    return high, middle, rest - middle


def stat_tile(top, total):
    lane = lax.broadcasted_iota(jnp.int32, (top.shape[0], 128), 1)
    top_high, top_middle, top_low = split3(top)
    total_high, total_middle, _ = split3(total)
    tile = jnp.where(lane == 4, total_middle, 0.0)
    tile = jnp.where(lane == 3, total_high, tile)
    tile = jnp.where(lane == 2, top_low, tile)
    tile = jnp.where(lane == 1, top_middle, tile)
    return jnp.where(lane == 0, top_high, tile)


def spread_stats(tile):
    source = lax.broadcasted_iota(jnp.int32, (128, 256), 0)
    target = lax.broadcasted_iota(jnp.int32, (128, 256), 1)
    is_top = (source < 3) & (target < 128)
    is_total = (source >= 3) & (source < 5) & (target >= 128)
    spread = jnp.where(is_top | is_total, 1.0, 0.0).astype(BF)
    both = dot(tile.astype(BF), spread, NN)
    return both[:, :128], both[:, 128:]


def join(parts):
    stats = [spread_stats(tile) for _, tile in parts]
    top = functools.reduce(jnp.maximum, [m for m, _ in stats])
    factors = [jnp.exp2((m - top) * FACTOR) for m, _ in stats]
    total = sum(f * l for f, (_, l) in zip(factors, stats))
    tiles = []
    for t in range(DC // 128):
        tiles.append(sum(f * data(t) for f, (data, _) in zip(factors, parts)))
    return tiles, top, total


def block_part(ref, index, count):
    rows = count * 16

    def data(t):
        return ref[index][..., 128 * t : 128 * t + 128].astype(F32).reshape(rows, 128)

    return data, ref[index][..., DC:WIDE].reshape(rows, 128)


def kernel(
    lengths_ref, positions_ref, query_ref, key_ref, value_ref, weight_hbm, cache_hbm, out_ref,
    cache, weight, wide, wide_sib, gathered, query_f32, scores_a, scores_b, probs_a, probs_b,
    stats_a, stats_b, partial, pair_send, pair_recv, first_send, first_recv, second_send, second_recv,
    latent, values, values_sib, out_send, out_first, out_mid, out_second, out_pairs, out_third,
    cache_sem, weight_sem, g1_send, g1_recv, g2_send, g2_recv, g3_send, g3_recv, g4_send, g4_recv,
    pair_ss, pair_rs, r1_send, r1_recv, r2_send, r2_recv, w_send, w_recv, v_send, v_recv,
    o1_send, o1_recv, o2_send, o2_recv, o3_send, o3_recv,
):
    kv = lax.axis_index("kv")
    row_y = lax.axis_index("head")
    x, z, core = kv // 8, (kv // 2) % 4, kv % 2

    def place(px, pz, pc, py):
        return (lax.rem(px, 4) * 8 + lax.rem(pz, 4) * 2 + pc, lax.rem(py, 4))

    def along_first(step):
        return place(x + step * (1 - core), z + step * core, core, row_y)

    def along_second(step):
        return place(x + step * core, z + step * (1 - core), core, row_y)

    def along_third(step):
        return place(x, z, core, row_y + step)

    sibling = place(x, z, 1 - core, row_y)

    def remote(src, dst, send, recv, device):
        return pltpu.make_async_remote_copy(
            src_ref=src, dst_ref=dst, send_sem=send, recv_sem=recv,
            device_id=device, device_id_type=MESH,
        )

    def cache_copy(b):
        return pltpu.make_async_copy(cache_hbm.at[b], cache.at[b], cache_sem.at[b])

    weight_copy = pltpu.make_async_copy(weight_hbm, weight, weight_sem.at[0])

    barrier = pltpu.get_barrier_semaphore()
    partners = [sibling]
    for step in range(1, 4):
        partners += [along_first(step), along_second(step), along_third(step)]
    for partner in partners:
        pl.semaphore_signal(barrier, inc=1, device_id=partner, device_id_type=MESH)
    weight_copy.start()
    for b in range(B):
        cache_copy(b).start()

    line = lax.broadcasted_iota(jnp.int32, (ROWS, ROWS), 0)
    column = lax.broadcasted_iota(jnp.int32, (ROWS, ROWS), 1)
    reorder = jnp.where(column == (line % S) * B + line // S, 1.0, 0.0).astype(BF)
    query = dot(reorder, query_ref[...], NN)
    query_latent = dot(query[:, :DN].astype(BF), key_ref[...], NN)
    lane = lax.broadcasted_iota(jnp.int32, (ROWS, DR // 2), 1).astype(F32)
    frequency = jnp.exp(lane * (-np.log(10000.0) / (DR // 2)))
    token_row = lax.broadcasted_iota(jnp.int32, (ROWS, DR // 2), 0)
    spot = jnp.zeros((ROWS, DR // 2), jnp.int32)
    for b in range(B):
        spot = jnp.where(token_row // S == b, positions_ref[b], spot)
    angle = (spot + token_row % S).astype(F32) * frequency
    cosine, sine = jnp.cos(angle), jnp.sin(angle)
    first_half, second_half = query[:, DN : DN + DR // 2], query[:, DN + DR // 2 :]
    own = jnp.concatenate(
        [
            query_latent,
            first_half * cosine - second_half * sine,
            second_half * cosine + first_half * sine,
            jnp.zeros((ROWS, WIDE - RANK), F32),
        ],
        axis=1,
    ).astype(BF)
    for k in range(CHUNKS):
        gathered[0, k, 0] = own[16 * k : 16 * k + 16]

    pl.semaphore_wait(barrier, len(partners))

    def gather_one(k, step):
        return remote(
            gathered.at[0, k, 0], gathered.at[0, k, step],
            g1_send.at[k, step - 1], g1_recv.at[k, step - 1], along_first(step),
        )

    def gather_two(k, side):
        return remote(
            gathered.at[0, k, pl.ds(0, 4)], gathered.at[0, k, pl.ds(4 if side == 0 else 12, 4)],
            g2_send.at[k, side], g2_recv.at[k, side], along_second(1 if side == 0 else 3),
        )

    def gather_three(k, side):
        return remote(
            gathered.at[0, k, pl.ds(4 if side == 0 else 14, 2)],
            gathered.at[0, k, pl.ds(8 if side == 0 else 10, 2)],
            g3_send.at[k, side], g3_recv.at[k, side], along_second(1 if side == 0 else 3),
        )

    def gather_four(k):
        return remote(gathered.at[0, k], gathered.at[1, k], g4_send.at[k], g4_recv.at[k], sibling)

    for k in range(CHUNKS):
        for step in range(1, 4):
            gather_one(k, step).start()

    weight_copy.wait()

    def widen(g, carry):
        base = pl.multiple_of(g * (16 * FEAT), 128)
        strip = weight[:, pl.ds(base, 16 * FEAT)]
        gap = jnp.zeros((DN, 64 - FEAT), BF)
        for low in range(2):
            wx, wz = g // 2, (g % 2) * 2 + low
            for parity in range(2):
                slot = wz * 4 + wx if parity == 0 else wx * 4 + wz
                for half in range(2):
                    start = ((low * 2 + parity) * 4 + half * 2) * FEAT
                    wide[parity, slot, :, 128 * half : 128 * half + 128] = jnp.concatenate(
                        [strip[:, start : start + FEAT], gap,
                         strip[:, start + FEAT : start + 2 * FEAT], gap], axis=1)
        return carry

    lax.fori_loop(0, 8, widen, 0)
    weight_send = remote(wide.at[1 - core], wide_sib, w_send.at[0], w_recv.at[0], sibling)

    for k in range(CHUNKS):
        for step in range(1, 4):
            gather_one(k, step).wait_recv()
        for side in range(2):
            gather_two(k, side).start()
    for k in range(CHUNKS):
        for side in range(2):
            gather_two(k, side).wait_recv()
            gather_three(k, side).start()
    for k in range(CHUNKS):
        for side in range(2):
            gather_three(k, side).wait_recv()
        gather_four(k).start()
    weight_send.start()

    def unpack(k):
        for parity in range(2):
            for t in range(WIDE // 128):
                query_f32[k, t, parity * 256 : parity * 256 + 256] = (
                    gathered[parity, k, :, :, 128 * t : 128 * t + 128].astype(F32).reshape(256, 128)
                )

    for k in range(CHUNKS):
        gather_four(k).wait_recv()
        unpack(k)

    slots = lax.broadcasted_iota(jnp.int32, (1, SHARD), 1)

    def score(b, target):
        rows = []
        for s in range(S):
            r = b * S + s
            tiles = [
                query_f32[r // 16, t, pl.ds(r % 16, 32, stride=16), :] for t in range(WIDE // 128)
            ]
            rows.append(jnp.concatenate(tiles, axis=1)[:, :RANK])
        target[...] = dot(jnp.concatenate(rows, axis=0).astype(BF), cache[b], NN)

    def soften(b, source, target, stats):
        for s in range(S):
            last = lengths_ref[b] - S + s - kv * SHARD
            part = jnp.where(slots <= last, source[32 * s : 32 * s + 32, :], MASKED)
            top = jnp.max(part, axis=1, keepdims=True)
            weights = jnp.exp2((part - top) * FACTOR)
            total = jnp.sum(weights, axis=1, keepdims=True)
            target[32 * s : 32 * s + 32, :] = weights.astype(BF)
            stats[32 * s : 32 * s + 32, :] = stat_tile(top, total)

    def weigh(b, source, stats):
        numerators = dot(source[...], cache[b, :DC], NT)
        for s in range(S):
            r = b * S + s
            for t in range(DC // 128):
                partial[r // 16, t, pl.ds(r % 16, 32, stride=16), :] = numerators[
                    32 * s : 32 * s + 32, 128 * t : 128 * t + 128
                ]
            partial[r // 16, 4, pl.ds(r % 16, 32, stride=16), :] = stats[32 * s : 32 * s + 32, :]

    def pair_copy(k):
        return remote(pair_send.at[k], pair_recv.at[k], pair_ss.at[k], pair_rs.at[k], sibling)

    def first_copy(k, step):
        return remote(
            first_send.at[k, pl.ds(4 * step, 4)], first_recv.at[k, step - 1],
            r1_send.at[k, step - 1], r1_recv.at[k, step - 1], along_second(4 - step),
        )

    def second_copy(k, step):
        return remote(
            second_send.at[k, step], second_recv.at[k, step - 1],
            r2_send.at[k, step - 1], r2_recv.at[k, step - 1], along_first(4 - step),
        )

    def step_pair(k):
        for t in range(WIDE // 128):
            pair_send[k, :, :, 128 * t : 128 * t + 128] = (
                partial[k, t, 256:512].astype(BF).reshape(16, 16, 128)
            )
        pair_copy(k).start()

    def step_first(k):
        pair_copy(k).wait_recv()
        for group in range(4):
            rows = slice(64 * group, 64 * group + 64)
            own_part = (lambda t, rows=rows: partial[k, t, rows], partial[k, 4, rows])
            span = slice(4 * group, 4 * group + 4)
            store_group(k, group, join([own_part, block_part(pair_recv, (k, span), 4)]))
        for step in (2, 1, 3):
            first_copy(k, step).start()

    def store_group(k, group, joined):
        tiles, top, total = joined
        tiles = tiles + [stat_tile(top, total)]
        for t in range(WIDE // 128):
            first_send[k, 4 * group : 4 * group + 4, :, 128 * t : 128 * t + 128] = (
                tiles[t].astype(BF).reshape(4, 16, 128)
            )

    def step_second(k):
        for step in range(1, 4):
            first_copy(k, step).wait_recv()
        parts = [block_part(first_send, (k, slice(0, 4)), 4)]
        parts += [block_part(first_recv, (k, step), 4) for step in range(3)]
        tiles, top, total = join(parts)
        tiles = tiles + [stat_tile(top, total)]
        for t in range(WIDE // 128):
            second_send[k, :, :, 128 * t : 128 * t + 128] = tiles[t].astype(BF).reshape(4, 16, 128)
        for step in (2, 1, 3):
            second_copy(k, step).start()

    def step_last(k):
        for step in range(1, 4):
            second_copy(k, step).wait_recv()
        parts = [block_part(second_send, (k, 0), 1)]
        parts += [block_part(second_recv, (k, step), 1) for step in range(3)]
        tiles, _, total = join(parts)
        for t in range(DC // 128):
            latent[16 * k : 16 * k + 16, 128 * t : 128 * t + 128] = (tiles[t] / total).astype(BF)

    cache_copy(0).wait()
    score(0, scores_a)
    soften(0, scores_a, probs_a, stats_a)

    def after(b, schedule):
        for when, step, k in schedule:
            pl.when(b == when)(functools.partial(step, k))

    def rollout_pair(i, carry):
        b = 2 * i
        cache_copy(b + 1).wait()
        cache_copy(b + 2).wait()
        score(b + 1, scores_b)
        weigh(b, probs_a, stats_a)
        soften(b + 1, scores_b, probs_b, stats_b)
        after(b, [(10, step_pair, 1), (12, step_first, 1)])
        score(b + 2, scores_a)
        weigh(b + 1, probs_b, stats_b)
        soften(b + 2, scores_a, probs_a, stats_a)
        after(b + 1, [(5, step_pair, 0), (7, step_first, 0), (9, step_second, 0), (13, step_last, 0)])
        return carry

    lax.fori_loop(0, B // 2 - 1, rollout_pair, 0)
    cache_copy(B - 1).wait()
    score(B - 1, scores_b)
    weigh(B - 2, probs_a, stats_a)
    soften(B - 1, scores_b, probs_b, stats_b)
    step_second(1)
    weigh(B - 1, probs_b, stats_b)
    step_pair(2)
    step_last(1)
    step_first(2)
    step_second(2)
    step_last(2)

    head_values = dot(latent[...], value_ref[...], NN).astype(BF)
    back = jnp.where(line == (column % S) * B + column // S, 1.0, 0.0).astype(BF)
    values[...] = dot(back, head_values, NN).astype(BF)
    values_copy = remote(values, values_sib, v_send.at[0], v_recv.at[0], sibling)
    values_copy.start()
    weight_send.wait_recv()
    values_copy.wait_recv()

    own_second = x * core + z * (1 - core)
    own_first = x * (1 - core) + z * core
    both_values = jnp.concatenate([values[...], values_sib[...]], axis=1)

    def project(t, carry):
        both_weights = jnp.concatenate([wide[core, t], wide_sib[t]], axis=0)
        out_send[t] = dot(both_values, both_weights, NN).astype(BF)
        return carry

    lax.fori_loop(0, 16, project, 0)

    def out_one(step):
        return remote(
            out_send.at[pl.ds(4 * lax.rem(own_second + step, 4), 4)], out_first.at[step - 1],
            o1_send.at[step - 1], o1_recv.at[step - 1], along_second(step),
        )

    def out_two(step):
        return remote(
            out_mid.at[lax.rem(own_first + step, 4)], out_second.at[step - 1],
            o2_send.at[step - 1], o2_recv.at[step - 1], along_first(step),
        )

    def out_three(step):
        return remote(
            out_pairs.at[lax.rem(row_y + step, 4) // 2], out_third.at[step - 1],
            o3_send.at[step - 1], o3_recv.at[step - 1], along_third(step),
        )

    for step in (2, 1, 3):
        out_one(step).start()
    for step in range(1, 4):
        out_one(step).wait_recv()
    for f in range(4):
        total = out_send[own_second * 4 + f].astype(F32)
        for step in range(3):
            total = total + out_first[step, f].astype(F32)
        out_mid[f] = total.astype(BF)
    for step in (2, 1, 3):
        out_two(step).start()
    for step in range(1, 4):
        out_two(step).wait_recv()
    total = out_mid[own_first].astype(F32)
    for step in range(3):
        total = total + out_second[step].astype(F32)
    out_pairs[0] = total[:, :128].astype(BF)
    out_pairs[1] = total[:, 128:].astype(BF)
    for step in (2, 1, 3):
        out_three(step).start()
    for step in range(1, 4):
        out_three(step).wait_recv()
    total = out_pairs[row_y // 2].astype(F32)
    for step in range(3):
        total = total + out_third[step].astype(F32)
    mine = jnp.where(row_y % 2 == 0, total[:, :FEAT], total[:, 64 : 64 + FEAT])
    out_ref[...] = mine.astype(BF)

    for k in range(CHUNKS):
        for step in range(1, 4):
            gather_one(k, step).wait_send()
            first_copy(k, step).wait_send()
            second_copy(k, step).wait_send()
        for side in range(2):
            gather_two(k, side).wait_send()
            gather_three(k, side).wait_send()
        gather_four(k).wait_send()
        pair_copy(k).wait_send()
    weight_send.wait_send()
    values_copy.wait_send()
    for step in range(1, 4):
        out_one(step).wait_send()
        out_two(step).wait_send()
        out_three(step).wait_send()


def body(query_heads, key_up, value_up, output_weight, latent_cache, lengths, positions):
    query = jnp.transpose(query_heads[:, :, 0, :], (1, 0, 2)).reshape(ROWS, DN + DR)
    cache = jnp.swapaxes(latent_cache, 1, 2)
    width = output_weight.shape[1]
    dma = pltpu.SemaphoreType.DMA
    vmem, smem = pltpu.VMEM, pltpu.SMEM
    out = pl.pallas_call(
        kernel,
        out_shape=jax.ShapeDtypeStruct((ROWS, FEAT), BF),
        in_specs=[
            pl.BlockSpec(memory_space=smem),
            pl.BlockSpec(memory_space=smem),
            pl.BlockSpec(memory_space=vmem),
            pl.BlockSpec(memory_space=vmem),
            pl.BlockSpec(memory_space=vmem),
            pl.BlockSpec(memory_space=pl.ANY),
            pl.BlockSpec(memory_space=pl.ANY),
        ],
        out_specs=pl.BlockSpec(memory_space=vmem),
        scratch_shapes=[
            vmem((B, RANK, SHARD), BF),
            vmem((DN, width), BF),
            vmem((2, 16, DN, 256), BF),
            vmem((16, DN, 256), BF),
            vmem((2, CHUNKS, 16, 16, WIDE), BF),
            vmem((CHUNKS, WIDE // 128, 512, 128), F32),
            vmem((96, SHARD), F32),
            vmem((96, SHARD), F32),
            vmem((96, SHARD), BF),
            vmem((96, SHARD), BF),
            vmem((96, 128), F32),
            vmem((96, 128), F32),
            vmem((CHUNKS, WIDE // 128, 512, 128), F32),
            vmem((CHUNKS, 16, 16, WIDE), BF),
            vmem((CHUNKS, 16, 16, WIDE), BF),
            vmem((CHUNKS, 16, 16, WIDE), BF),
            vmem((CHUNKS, 3, 4, 16, WIDE), BF),
            vmem((CHUNKS, 4, 16, WIDE), BF),
            vmem((CHUNKS, 3, 16, WIDE), BF),
            vmem((ROWS, DC), BF),
            vmem((ROWS, 128), BF),
            vmem((ROWS, 128), BF),
            vmem((16, ROWS, 256), BF),
            vmem((3, 4, ROWS, 256), BF),
            vmem((4, ROWS, 256), BF),
            vmem((3, ROWS, 256), BF),
            vmem((2, ROWS, 128), BF),
            vmem((3, ROWS, 128), BF),
            dma((B,)),
            dma((1,)),
            dma((CHUNKS, 3)), dma((CHUNKS, 3)),
            dma((CHUNKS, 2)), dma((CHUNKS, 2)),
            dma((CHUNKS, 2)), dma((CHUNKS, 2)),
            dma((CHUNKS,)), dma((CHUNKS,)),
            dma((CHUNKS,)), dma((CHUNKS,)),
            dma((CHUNKS, 3)), dma((CHUNKS, 3)),
            dma((CHUNKS, 3)), dma((CHUNKS, 3)),
            dma((1,)), dma((1,)),
            dma((1,)), dma((1,)),
            dma((3,)), dma((3,)),
            dma((3,)), dma((3,)),
            dma((3,)), dma((3,)),
        ],
        compiler_params=pltpu.CompilerParams(
            collective_id=0, has_side_effects=True, vmem_limit_bytes=56 * 2**20
        ),
    )(lengths, positions, query, key_up[0], value_up[0], output_weight, cache)
    return jnp.transpose(out.reshape(S, B, FEAT), (1, 0, 2))


def solution(mesh):
    in_specs = (
        P(None, None, ("kv", "head"), None),
        P(("kv", "head"), None, None),
        P(("kv", "head"), None, None),
        P(("kv", "head"), None),
        P(None, "kv", None),
        P(),
        P(),
    )
    out_specs = P(None, None, ("kv", "head"))
    return jax.shard_map(body, mesh=mesh, in_specs=in_specs, out_specs=out_specs, check_vma=False)
```

```python
import functools

import jax
import jax.numpy as jnp
import numpy as np
from jax import lax
from jax.experimental import pallas as pl
from jax.experimental.pallas import tpu as pltpu
from jax.sharding import PartitionSpec as P

MESH = pl.DeviceIdType.MESH
BF = jnp.bfloat16
F32 = jnp.float32

DN = 128
DR = 64
DC = 512
B = 16
S = 3
ROWS = B * S
CHUNKS = ROWS // 16
RANK = DC + DR
WIDE = 640
SHARD = 1024
FEAT = 56
MASKED = -(2.0**100)
FACTOR = float(np.log2(np.e) / np.sqrt(DN + DR))

dot = functools.partial(lax.dot_general, preferred_element_type=F32)
NN = (((1,), (0,)), ((), ()))
NT = (((1,), (1,)), ((), ()))


def split3(value):
    high = value.astype(BF).astype(F32)
    rest = value - high
    middle = rest.astype(BF).astype(F32)
    return high, middle, rest - middle


def stat_tile(top, total):
    lane = lax.broadcasted_iota(jnp.int32, (top.shape[0], 128), 1)
    top_high, top_middle, top_low = split3(top)
    total_high, total_middle, _ = split3(total)
    tile = jnp.where(lane == 4, total_middle, 0.0)
    tile = jnp.where(lane == 3, total_high, tile)
    tile = jnp.where(lane == 2, top_low, tile)
    tile = jnp.where(lane == 1, top_middle, tile)
    return jnp.where(lane == 0, top_high, tile)


def spread_matrix():
    source = lax.broadcasted_iota(jnp.int32, (128, 256), 0)
    target = lax.broadcasted_iota(jnp.int32, (128, 256), 1)
    is_top = (source < 3) & (target < 128)
    is_total = (source >= 3) & (source < 5) & (target >= 128)
    return jnp.where(is_top | is_total, 1.0, 0.0).astype(BF)


def spread_stats(tile, spread):
    both = dot(tile.astype(BF), spread[...], NN)
    return both[:, :128], both[:, 128:]


def join(parts, spread):
    stats = [spread_stats(tile, spread) for _, tile in parts]
    top = functools.reduce(jnp.maximum, [m for m, _ in stats])
    factors = [jnp.exp2((m - top) * FACTOR) for m, _ in stats]
    total = sum(f * l for f, (_, l) in zip(factors, stats))
    tiles = []
    for t in range(DC // 128):
        tiles.append(sum(f * data(t) for f, (data, _) in zip(factors, parts)))
    return tiles, top, total


def block_part(ref, index, count):
    rows = count * 16

    def data(t):
        return ref[index][..., 128 * t : 128 * t + 128].astype(F32).reshape(rows, 128)

    return data, ref[index][..., DC:WIDE].reshape(rows, 128)


def kernel(
    lengths_ref, positions_ref, query_ref, key_ref, value_ref, weight_hbm, cache_hbm, out_ref,
    cache, weight, wide, wide_sib, gathered, query_f32, scores_a, scores_b, probs_a, probs_b,
    stats_a, stats_b, partial, pair_send, pair_recv, first_send, first_recv, second_send, second_recv,
    latent, values, values_sib, out_send, out_first, out_mid, out_second, out_pairs, out_third,
    spread, cache_sem, weight_sem, g1_send, g1_recv, g2_send, g2_recv, g3_send, g3_recv, g4_send, g4_recv,
    pair_ss, pair_rs, r1_send, r1_recv, r2_send, r2_recv, w_send, w_recv, v_send, v_recv,
    o1_send, o1_recv, o2_send, o2_recv, o3_send, o3_recv,
):
    kv = lax.axis_index("kv")
    row_y = lax.axis_index("head")
    x, z, core = kv // 8, (kv // 2) % 4, kv % 2

    def place(px, pz, pc, py):
        return (lax.rem(px, 4) * 8 + lax.rem(pz, 4) * 2 + pc, lax.rem(py, 4))

    def along_first(step):
        return place(x + step * (1 - core), z + step * core, core, row_y)

    def along_second(step):
        return place(x + step * core, z + step * (1 - core), core, row_y)

    def along_third(step):
        return place(x, z, core, row_y + step)

    sibling = place(x, z, 1 - core, row_y)

    def remote(src, dst, send, recv, device):
        return pltpu.make_async_remote_copy(
            src_ref=src, dst_ref=dst, send_sem=send, recv_sem=recv,
            device_id=device, device_id_type=MESH,
        )

    def cache_copy(b):
        return pltpu.make_async_copy(cache_hbm.at[b], cache.at[b], cache_sem.at[b])

    weight_copy = pltpu.make_async_copy(weight_hbm, weight, weight_sem.at[0])

    barrier = pltpu.get_barrier_semaphore()
    partners = [sibling]
    for step in range(1, 4):
        partners += [along_first(step), along_second(step), along_third(step)]
    for partner in partners:
        pl.semaphore_signal(barrier, inc=1, device_id=partner, device_id_type=MESH)
    weight_copy.start()
    for b in range(B):
        cache_copy(b).start()

    spread[...] = spread_matrix()

    line = lax.broadcasted_iota(jnp.int32, (ROWS, ROWS), 0)
    column = lax.broadcasted_iota(jnp.int32, (ROWS, ROWS), 1)
    reorder = jnp.where(column == (line % S) * B + line // S, 1.0, 0.0).astype(BF)
    query = dot(reorder, query_ref[...], NN)
    query_latent = dot(query[:, :DN].astype(BF), key_ref[...], NN)
    lane = lax.broadcasted_iota(jnp.int32, (ROWS, DR // 2), 1).astype(F32)
    frequency = jnp.exp(lane * (-np.log(10000.0) / (DR // 2)))
    token_row = lax.broadcasted_iota(jnp.int32, (ROWS, DR // 2), 0)
    spot = jnp.zeros((ROWS, DR // 2), jnp.int32)
    for b in range(B):
        spot = jnp.where(token_row // S == b, positions_ref[b], spot)
    angle = (spot + token_row % S).astype(F32) * frequency
    cosine, sine = jnp.cos(angle), jnp.sin(angle)
    first_half, second_half = query[:, DN : DN + DR // 2], query[:, DN + DR // 2 :]
    own = jnp.concatenate(
        [
            query_latent,
            first_half * cosine - second_half * sine,
            second_half * cosine + first_half * sine,
            jnp.zeros((ROWS, WIDE - RANK), F32),
        ],
        axis=1,
    ).astype(BF)
    for k in range(CHUNKS):
        gathered[0, k, 0] = own[16 * k : 16 * k + 16]

    pl.semaphore_wait(barrier, len(partners))

    def gather_one(k, step):
        return remote(
            gathered.at[0, k, 0], gathered.at[0, k, step],
            g1_send.at[k, step - 1], g1_recv.at[k, step - 1], along_first(step),
        )

    def gather_two(k, side):
        return remote(
            gathered.at[0, k, pl.ds(0, 4)], gathered.at[0, k, pl.ds(4 if side == 0 else 12, 4)],
            g2_send.at[k, side], g2_recv.at[k, side], along_second(1 if side == 0 else 3),
        )

    def gather_three(k, side):
        return remote(
            gathered.at[0, k, pl.ds(4 if side == 0 else 14, 2)],
            gathered.at[0, k, pl.ds(8 if side == 0 else 10, 2)],
            g3_send.at[k, side], g3_recv.at[k, side], along_second(1 if side == 0 else 3),
        )

    def gather_four(k):
        return remote(gathered.at[0, k], gathered.at[1, k], g4_send.at[k], g4_recv.at[k], sibling)

    for k in range(CHUNKS):
        for step in range(1, 4):
            gather_one(k, step).start()

    weight_copy.wait()

    def widen(g, carry):
        base = pl.multiple_of(g * (16 * FEAT), 128)
        strip = weight[:, pl.ds(base, 16 * FEAT)]
        gap = jnp.zeros((DN, 64 - FEAT), BF)
        for low in range(2):
            wx, wz = g // 2, (g % 2) * 2 + low
            for parity in range(2):
                slot = wz * 4 + wx if parity == 0 else wx * 4 + wz
                for half in range(2):
                    start = ((low * 2 + parity) * 4 + half * 2) * FEAT
                    wide[parity, slot, :, 128 * half : 128 * half + 128] = jnp.concatenate(
                        [strip[:, start : start + FEAT], gap,
                         strip[:, start + FEAT : start + 2 * FEAT], gap], axis=1)
        return carry

    lax.fori_loop(0, 8, widen, 0)
    weight_send = remote(wide.at[1 - core], wide_sib, w_send.at[0], w_recv.at[0], sibling)

    def to_second(k):
        for step in range(1, 4):
            gather_one(k, step).wait_recv()
        for side in range(2):
            gather_two(k, side).start()

    def to_third(k):
        for side in range(2):
            gather_two(k, side).wait_recv()
            gather_three(k, side).start()

    def to_sibling(k):
        for side in range(2):
            gather_three(k, side).wait_recv()
        gather_four(k).start()

    def unpack(k):
        for parity in range(2):
            for t in range(WIDE // 128):
                query_f32[k, t, parity * 256 : parity * 256 + 256] = (
                    gathered[parity, k, :, :, 128 * t : 128 * t + 128].astype(F32).reshape(256, 128)
                )

    def arrive(k):
        gather_four(k).wait_recv()
        unpack(k)

    to_second(0)
    to_second(1)
    to_third(0)
    to_second(2)
    to_third(1)
    to_sibling(0)
    to_third(2)
    weight_send.start()
    arrive(0)

    slots = lax.broadcasted_iota(jnp.int32, (1, SHARD), 1)

    def score(b, target):
        rows = []
        for s in range(S):
            r = b * S + s
            tiles = [
                query_f32[r // 16, t, pl.ds(r % 16, 32, stride=16), :] for t in range(WIDE // 128)
            ]
            rows.append(jnp.concatenate(tiles, axis=1)[:, :RANK])
        target[...] = dot(jnp.concatenate(rows, axis=0).astype(BF), cache[b], NN)

    def soften(b, source, target, stats):
        for s in range(S):
            last = lengths_ref[b] - S + s - kv * SHARD
            part = jnp.where(slots <= last, source[32 * s : 32 * s + 32, :], MASKED)
            top = jnp.max(part, axis=1, keepdims=True)
            weights = jnp.exp2((part - top) * FACTOR)
            total = jnp.sum(weights, axis=1, keepdims=True)
            target[32 * s : 32 * s + 32, :] = weights.astype(BF)
            stats[32 * s : 32 * s + 32, :] = stat_tile(top, total)

    def weigh(b, source, stats):
        numerators = dot(source[...], cache[b, :DC], NT)
        for s in range(S):
            r = b * S + s
            for t in range(DC // 128):
                partial[r // 16, t, pl.ds(r % 16, 32, stride=16), :] = numerators[
                    32 * s : 32 * s + 32, 128 * t : 128 * t + 128
                ]
            partial[r // 16, 4, pl.ds(r % 16, 32, stride=16), :] = stats[32 * s : 32 * s + 32, :]

    def pair_copy(k):
        return remote(pair_send.at[k], pair_recv.at[k], pair_ss.at[k], pair_rs.at[k], sibling)

    def first_copy(k, step):
        return remote(
            first_send.at[k, pl.ds(4 * step, 4)], first_recv.at[k, step - 1],
            r1_send.at[k, step - 1], r1_recv.at[k, step - 1], along_second(4 - step),
        )

    def second_copy(k, step):
        return remote(
            second_send.at[k, step], second_recv.at[k, step - 1],
            r2_send.at[k, step - 1], r2_recv.at[k, step - 1], along_first(4 - step),
        )

    def step_pair(k):
        for t in range(WIDE // 128):
            pair_send[k, :, :, 128 * t : 128 * t + 128] = (
                partial[k, t, 256:512].astype(BF).reshape(16, 16, 128)
            )
        pair_copy(k).start()

    def step_first(k):
        pair_copy(k).wait_recv()
        for group in range(4):
            rows = slice(64 * group, 64 * group + 64)
            own_part = (lambda t, rows=rows: partial[k, t, rows], partial[k, 4, rows])
            span = slice(4 * group, 4 * group + 4)
            store_group(k, group, join([own_part, block_part(pair_recv, (k, span), 4)], spread))
        for step in (2, 1, 3):
            first_copy(k, step).start()

    def store_group(k, group, joined):
        tiles, top, total = joined
        tiles = tiles + [stat_tile(top, total)]
        for t in range(WIDE // 128):
            first_send[k, 4 * group : 4 * group + 4, :, 128 * t : 128 * t + 128] = (
                tiles[t].astype(BF).reshape(4, 16, 128)
            )

    def step_second(k):
        for step in range(1, 4):
            first_copy(k, step).wait_recv()
        parts = [block_part(first_send, (k, slice(0, 4)), 4)]
        parts += [block_part(first_recv, (k, step), 4) for step in range(3)]
        tiles, top, total = join(parts, spread)
        tiles = tiles + [stat_tile(top, total)]
        for t in range(WIDE // 128):
            second_send[k, :, :, 128 * t : 128 * t + 128] = tiles[t].astype(BF).reshape(4, 16, 128)
        for step in (2, 1, 3):
            second_copy(k, step).start()

    def step_last(k):
        for step in range(1, 4):
            second_copy(k, step).wait_recv()
        parts = [block_part(second_send, (k, 0), 1)]
        parts += [block_part(second_recv, (k, step), 1) for step in range(3)]
        tiles, _, total = join(parts, spread)
        for t in range(DC // 128):
            latent[16 * k : 16 * k + 16, 128 * t : 128 * t + 128] = (tiles[t] / total).astype(BF)

    cache_copy(0).wait()
    score(0, scores_a)
    soften(0, scores_a, probs_a, stats_a)

    def after(b, schedule):
        for when, step, k in schedule:
            pl.when(b == when)(functools.partial(step, k))

    def rollout_pair(i, carry):
        b = 2 * i
        cache_copy(b + 1).wait()
        cache_copy(b + 2).wait()
        score(b + 1, scores_b)
        weigh(b, probs_a, stats_a)
        soften(b + 1, scores_b, probs_b, stats_b)
        after(b, [(0, to_sibling, 1), (2, to_sibling, 2), (8, arrive, 2), (8, step_first, 0), (10, step_pair, 1)])
        score(b + 2, scores_a)
        weigh(b + 1, probs_b, stats_b)
        soften(b + 2, scores_a, probs_a, stats_a)
        after(b + 1, [(3, arrive, 1), (5, step_pair, 0), (13, step_first, 1)])
        return carry

    lax.fori_loop(0, B // 2 - 1, rollout_pair, 0)
    cache_copy(B - 1).wait()
    score(B - 1, scores_b)
    weigh(B - 2, probs_a, stats_a)
    soften(B - 1, scores_b, probs_b, stats_b)
    weigh(B - 1, probs_b, stats_b)
    step_pair(2)
    step_second(0)
    step_first(2)
    step_second(1)
    step_last(0)
    step_second(2)
    step_last(1)
    step_last(2)

    head_values = dot(latent[...], value_ref[...], NN).astype(BF)
    back = jnp.where(line == (column % S) * B + column // S, 1.0, 0.0).astype(BF)
    values[...] = dot(back, head_values, NN).astype(BF)
    values_copy = remote(values, values_sib, v_send.at[0], v_recv.at[0], sibling)
    values_copy.start()
    weight_send.wait_recv()
    values_copy.wait_recv()

    own_second = x * core + z * (1 - core)
    own_first = x * (1 - core) + z * core
    both_values = jnp.concatenate([values[...], values_sib[...]], axis=1)

    def project(t, carry):
        both_weights = jnp.concatenate([wide[core, t], wide_sib[t]], axis=0)
        out_send[t] = dot(both_values, both_weights, NN).astype(BF)
        return carry

    lax.fori_loop(0, 16, project, 0)

    def out_one(step):
        return remote(
            out_send.at[pl.ds(4 * lax.rem(own_second + step, 4), 4)], out_first.at[step - 1],
            o1_send.at[step - 1], o1_recv.at[step - 1], along_second(step),
        )

    def out_two(step):
        return remote(
            out_mid.at[lax.rem(own_first + step, 4)], out_second.at[step - 1],
            o2_send.at[step - 1], o2_recv.at[step - 1], along_first(step),
        )

    def out_three(step):
        return remote(
            out_pairs.at[lax.rem(row_y + step, 4) // 2], out_third.at[step - 1],
            o3_send.at[step - 1], o3_recv.at[step - 1], along_third(step),
        )

    for step in (2, 1, 3):
        out_one(step).start()
    for step in range(1, 4):
        out_one(step).wait_recv()
    for f in range(4):
        total = out_send[own_second * 4 + f].astype(F32)
        for step in range(3):
            total = total + out_first[step, f].astype(F32)
        out_mid[f] = total.astype(BF)
    for step in (2, 1, 3):
        out_two(step).start()
    for step in range(1, 4):
        out_two(step).wait_recv()
    total = out_mid[own_first].astype(F32)
    for step in range(3):
        total = total + out_second[step].astype(F32)
    out_pairs[0] = total[:, :128].astype(BF)
    out_pairs[1] = total[:, 128:].astype(BF)
    for step in (2, 1, 3):
        out_three(step).start()
    for step in range(1, 4):
        out_three(step).wait_recv()
    total = out_pairs[row_y // 2].astype(F32)
    for step in range(3):
        total = total + out_third[step].astype(F32)
    mine = jnp.where(row_y % 2 == 0, total[:, :FEAT], total[:, 64 : 64 + FEAT])
    out_ref[...] = mine.astype(BF)

    for k in range(CHUNKS):
        for step in range(1, 4):
            gather_one(k, step).wait_send()
            first_copy(k, step).wait_send()
            second_copy(k, step).wait_send()
        for side in range(2):
            gather_two(k, side).wait_send()
            gather_three(k, side).wait_send()
        gather_four(k).wait_send()
        pair_copy(k).wait_send()
    weight_send.wait_send()
    values_copy.wait_send()
    for step in range(1, 4):
        out_one(step).wait_send()
        out_two(step).wait_send()
        out_three(step).wait_send()


def body(query_heads, key_up, value_up, output_weight, latent_cache, lengths, positions):
    query = jnp.transpose(query_heads[:, :, 0, :], (1, 0, 2)).reshape(ROWS, DN + DR)
    cache = jnp.swapaxes(latent_cache, 1, 2)
    width = output_weight.shape[1]
    dma = pltpu.SemaphoreType.DMA
    vmem, smem = pltpu.VMEM, pltpu.SMEM
    out = pl.pallas_call(
        kernel,
        out_shape=jax.ShapeDtypeStruct((ROWS, FEAT), BF),
        in_specs=[
            pl.BlockSpec(memory_space=smem),
            pl.BlockSpec(memory_space=smem),
            pl.BlockSpec(memory_space=vmem),
            pl.BlockSpec(memory_space=vmem),
            pl.BlockSpec(memory_space=vmem),
            pl.BlockSpec(memory_space=pl.ANY),
            pl.BlockSpec(memory_space=pl.ANY),
        ],
        out_specs=pl.BlockSpec(memory_space=vmem),
        scratch_shapes=[
            vmem((B, RANK, SHARD), BF),
            vmem((DN, width), BF),
            vmem((2, 16, DN, 256), BF),
            vmem((16, DN, 256), BF),
            vmem((2, CHUNKS, 16, 16, WIDE), BF),
            vmem((CHUNKS, WIDE // 128, 512, 128), F32),
            vmem((96, SHARD), F32),
            vmem((96, SHARD), F32),
            vmem((96, SHARD), BF),
            vmem((96, SHARD), BF),
            vmem((96, 128), F32),
            vmem((96, 128), F32),
            vmem((CHUNKS, WIDE // 128, 512, 128), F32),
            vmem((CHUNKS, 16, 16, WIDE), BF),
            vmem((CHUNKS, 16, 16, WIDE), BF),
            vmem((CHUNKS, 16, 16, WIDE), BF),
            vmem((CHUNKS, 3, 4, 16, WIDE), BF),
            vmem((CHUNKS, 4, 16, WIDE), BF),
            vmem((CHUNKS, 3, 16, WIDE), BF),
            vmem((ROWS, DC), BF),
            vmem((ROWS, 128), BF),
            vmem((ROWS, 128), BF),
            vmem((16, ROWS, 256), BF),
            vmem((3, 4, ROWS, 256), BF),
            vmem((4, ROWS, 256), BF),
            vmem((3, ROWS, 256), BF),
            vmem((2, ROWS, 128), BF),
            vmem((3, ROWS, 128), BF),
            vmem((128, 256), BF),
            dma((B,)),
            dma((1,)),
            dma((CHUNKS, 3)), dma((CHUNKS, 3)),
            dma((CHUNKS, 2)), dma((CHUNKS, 2)),
            dma((CHUNKS, 2)), dma((CHUNKS, 2)),
            dma((CHUNKS,)), dma((CHUNKS,)),
            dma((CHUNKS,)), dma((CHUNKS,)),
            dma((CHUNKS, 3)), dma((CHUNKS, 3)),
            dma((CHUNKS, 3)), dma((CHUNKS, 3)),
            dma((1,)), dma((1,)),
            dma((1,)), dma((1,)),
            dma((3,)), dma((3,)),
            dma((3,)), dma((3,)),
            dma((3,)), dma((3,)),
        ],
        compiler_params=pltpu.CompilerParams(
            collective_id=0, has_side_effects=True, vmem_limit_bytes=56 * 2**20
        ),
    )(lengths, positions, query, key_up[0], value_up[0], output_weight, cache)
    return jnp.transpose(out.reshape(S, B, FEAT), (1, 0, 2))


def solution(mesh):
    in_specs = (
        P(None, None, ("kv", "head"), None),
        P(("kv", "head"), None, None),
        P(("kv", "head"), None, None),
        P(("kv", "head"), None),
        P(None, "kv", None),
        P(),
        P(),
    )
    out_specs = P(None, None, ("kv", "head"))
    return jax.shard_map(body, mesh=mesh, in_specs=in_specs, out_specs=out_specs, check_vma=False)
```

```python
import functools

import jax
import jax.numpy as jnp
import numpy as np
from jax import lax
from jax.experimental import pallas as pl
from jax.experimental.pallas import tpu as pltpu
from jax.sharding import PartitionSpec as P

MESH = pl.DeviceIdType.MESH
BF = jnp.bfloat16
F32 = jnp.float32

DN = 128
DR = 64
DC = 512
B = 16
S = 3
ROWS = B * S
CHUNKS = ROWS // 16
RANK = DC + DR
WIDE = 640
SHARD = 1024
FEAT = 56
MASKED = -(2.0**100)
FACTOR = float(np.log2(np.e) / np.sqrt(DN + DR))

dot = functools.partial(lax.dot_general, preferred_element_type=F32)
NN = (((1,), (0,)), ((), ()))
NT = (((1,), (1,)), ((), ()))


def split3(value):
    high = value.astype(BF).astype(F32)
    rest = value - high
    middle = rest.astype(BF).astype(F32)
    return high, middle, rest - middle


def stat_tile(top, total):
    lane = lax.broadcasted_iota(jnp.int32, (top.shape[0], 128), 1)
    top_high, top_middle, top_low = split3(top)
    total_high, total_middle, _ = split3(total)
    tile = jnp.where(lane == 4, total_middle, 0.0)
    tile = jnp.where(lane == 3, total_high, tile)
    tile = jnp.where(lane == 2, top_low, tile)
    tile = jnp.where(lane == 1, top_middle, tile)
    return jnp.where(lane == 0, top_high, tile)


def spread_matrix():
    source = lax.broadcasted_iota(jnp.int32, (128, 256), 0)
    target = lax.broadcasted_iota(jnp.int32, (128, 256), 1)
    is_top = (source < 3) & (target < 128)
    is_total = (source >= 3) & (source < 5) & (target >= 128)
    return jnp.where(is_top | is_total, 1.0, 0.0).astype(BF)


def spread_stats(tile, spread):
    both = dot(tile.astype(BF), spread[...], NN)
    return both[:, :128], both[:, 128:]


def join(parts, spread):
    stats = [spread_stats(tile, spread) for _, tile in parts]
    top = functools.reduce(jnp.maximum, [m for m, _ in stats])
    factors = [jnp.exp2((m - top) * FACTOR) for m, _ in stats]
    total = sum(f * l for f, (_, l) in zip(factors, stats))
    tiles = []
    for t in range(DC // 128):
        tiles.append(sum(f * data(t) for f, (data, _) in zip(factors, parts)))
    return tiles, top, total


def block_part(ref, index, count):
    rows = count * 16

    def data(t):
        return ref[index][..., 128 * t : 128 * t + 128].astype(F32).reshape(rows, 128)

    return data, ref[index][..., DC:WIDE].reshape(rows, 128)


def kernel(
    lengths_ref, positions_ref, query_ref, key_ref, value_ref, weight_hbm, cache_hbm, out_ref,
    cache, weight, wide, weights_all, gathered, query_f32, scores_a, scores_b, probs_a, probs_b,
    stats_a, stats_b, partial, pair_send, pair_recv, first_send, first_recv, second_send, second_recv,
    latent, values, out_send, out_recv,
    spread, cache_sem, weight_sem, g1_send, g1_recv, g2_send, g2_recv, g3_send, g3_recv,
    pair_ss, pair_rs, r1_send, r1_recv, r2_send, r2_recv, w_send, w_recv, v_send, v_recv,
    o_send, o_recv,
):
    kv = lax.axis_index("kv")
    row_y = lax.axis_index("head")
    x, z, core = kv // 8, (kv // 2) % 4, kv % 2

    def place(px, pz, pc, py):
        return (lax.rem(px, 4) * 8 + lax.rem(pz, 4) * 2 + pc, lax.rem(py, 4))

    def along_first(step):
        return place(x + step * (1 - core), z + step * core, core, row_y)

    def along_second(step):
        return place(x + step * core, z + step * (1 - core), core, row_y)

    def column_peer(peer):
        return place(x, z, lax.rem(core + peer // 4, 2), row_y + peer % 4)

    def plane_peer(peer):
        return place(x + peer // 4, z + peer % 4, core, row_y)

    sibling = place(x, z, 1 - core, row_y)

    def remote(src, dst, send, recv, device):
        return pltpu.make_async_remote_copy(
            src_ref=src, dst_ref=dst, send_sem=send, recv_sem=recv,
            device_id=device, device_id_type=MESH,
        )

    def cache_copy(b):
        return pltpu.make_async_copy(cache_hbm.at[b], cache.at[b], cache_sem.at[b])

    weight_copy = pltpu.make_async_copy(weight_hbm, weight, weight_sem.at[0])

    barrier = pltpu.get_barrier_semaphore()
    partners = [column_peer(peer) for peer in range(1, 8)] + [plane_peer(peer) for peer in range(1, 16)]
    for partner in partners:
        pl.semaphore_signal(barrier, inc=1, device_id=partner, device_id_type=MESH)
    weight_copy.start()
    for b in range(B):
        cache_copy(b).start()

    spread[...] = spread_matrix()

    line = lax.broadcasted_iota(jnp.int32, (ROWS, ROWS), 0)
    column = lax.broadcasted_iota(jnp.int32, (ROWS, ROWS), 1)
    reorder = jnp.where(column == (line % S) * B + line // S, 1.0, 0.0).astype(BF)
    query = dot(reorder, query_ref[...], NN)
    query_latent = dot(query[:, :DN].astype(BF), key_ref[...], NN)
    lane = lax.broadcasted_iota(jnp.int32, (ROWS, DR // 2), 1).astype(F32)
    frequency = jnp.exp(lane * (-np.log(10000.0) / (DR // 2)))
    token_row = lax.broadcasted_iota(jnp.int32, (ROWS, DR // 2), 0)
    spot = jnp.zeros((ROWS, DR // 2), jnp.int32)
    for b in range(B):
        spot = jnp.where(token_row // S == b, positions_ref[b], spot)
    angle = (spot + token_row % S).astype(F32) * frequency
    cosine, sine = jnp.cos(angle), jnp.sin(angle)
    first_half, second_half = query[:, DN : DN + DR // 2], query[:, DN + DR // 2 :]
    own = jnp.concatenate(
        [
            query_latent,
            first_half * cosine - second_half * sine,
            second_half * cosine + first_half * sine,
            jnp.zeros((ROWS, WIDE - RANK), F32),
        ],
        axis=1,
    ).astype(BF)
    for k in range(CHUNKS):
        gathered[0, k, 0] = own[16 * k : 16 * k + 16]

    pl.semaphore_wait(barrier, len(partners))

    def gather_one(k, step):
        return remote(
            gathered.at[0, k, 0], gathered.at[0, k, step],
            g1_send.at[k, step - 1], g1_recv.at[k, step - 1], along_first(step),
        )

    def gather_two(k, step):
        return remote(
            gathered.at[0, k, pl.ds(0, 4)], gathered.at[0, k, pl.ds(4 * step, 4)],
            g2_send.at[k, step - 1], g2_recv.at[k, step - 1], along_second(step),
        )

    def gather_three(k, group):
        span = pl.ds(4 * group, 4)
        return remote(
            gathered.at[0, k, span], gathered.at[1, k, span],
            g3_send.at[k, group], g3_recv.at[k, group], sibling,
        )

    for k in range(CHUNKS):
        for step in range(1, 4):
            gather_one(k, step).start()

    weight_copy.wait()

    def widen(g, carry):
        base = pl.multiple_of(g * (16 * FEAT), 128)
        strip = weight[:, pl.ds(base, 16 * FEAT)]
        gap = jnp.zeros((DN, 64 - FEAT), BF)
        for parity in range(2):
            for side in range(4):
                start = (parity * 4 + side) * FEAT
                wide[parity, side, :, pl.ds(pl.multiple_of(g * 128, 128), 128)] = jnp.concatenate(
                    [strip[:, start : start + FEAT], gap,
                     strip[:, start + 8 * FEAT : start + 9 * FEAT], gap], axis=1)
        return carry

    lax.fori_loop(0, 8, widen, 0)

    def weight_send(peer):
        turn, step = peer // 4, peer % 4
        return remote(
            wide.at[lax.rem(core + turn, 2), lax.rem(row_y + step, 4)], weights_all.at[peer],
            w_send.at[peer - 1], w_recv.at[peer - 1], column_peer(peer),
        )

    for peer in range(1, 8):
        weight_send(peer).start()
    weights_all[0] = wide[core, row_y]

    def to_second(k):
        for step in range(1, 4):
            gather_one(k, step).wait_recv()
        for step in (2, 1, 3):
            gather_two(k, step).start()
        gather_three(k, 0).start()

    def to_sibling(k):
        for step in (1, 3, 2):
            gather_two(k, step).wait_recv()
            gather_three(k, step).start()

    def unpack(k):
        for parity in range(2):
            for t in range(WIDE // 128):
                query_f32[k, t, parity * 256 : parity * 256 + 256] = (
                    gathered[parity, k, :, :, 128 * t : 128 * t + 128].astype(F32).reshape(256, 128)
                )

    def arrive(k):
        for group in range(4):
            gather_three(k, group).wait_recv()
        unpack(k)

    to_second(0)
    to_second(1)
    to_sibling(0)
    to_second(2)
    arrive(0)

    slots = lax.broadcasted_iota(jnp.int32, (1, SHARD), 1)

    def score(b, target):
        rows = []
        for s in range(S):
            r = b * S + s
            tiles = [
                query_f32[r // 16, t, pl.ds(r % 16, 32, stride=16), :] for t in range(WIDE // 128)
            ]
            rows.append(jnp.concatenate(tiles, axis=1)[:, :RANK])
        target[...] = dot(jnp.concatenate(rows, axis=0).astype(BF), cache[b], NN)

    def soften(b, source, target, stats):
        for s in range(S):
            last = lengths_ref[b] - S + s - kv * SHARD
            part = jnp.where(slots <= last, source[32 * s : 32 * s + 32, :], MASKED)
            top = jnp.max(part, axis=1, keepdims=True)
            weights = jnp.exp2((part - top) * FACTOR)
            total = jnp.sum(weights, axis=1, keepdims=True)
            target[32 * s : 32 * s + 32, :] = weights.astype(BF)
            stats[32 * s : 32 * s + 32, :] = stat_tile(top, total)

    def weigh(b, source, stats):
        numerators = dot(source[...], cache[b, :DC], NT)
        for s in range(S):
            r = b * S + s
            for t in range(DC // 128):
                partial[r // 16, t, pl.ds(r % 16, 32, stride=16), :] = numerators[
                    32 * s : 32 * s + 32, 128 * t : 128 * t + 128
                ]
            partial[r // 16, 4, pl.ds(r % 16, 32, stride=16), :] = stats[32 * s : 32 * s + 32, :]

    def pair_copy(k):
        return remote(pair_send.at[k], pair_recv.at[k], pair_ss.at[k], pair_rs.at[k], sibling)

    def first_copy(k, step):
        return remote(
            first_send.at[k, pl.ds(4 * step, 4)], first_recv.at[k, step - 1],
            r1_send.at[k, step - 1], r1_recv.at[k, step - 1], along_second(4 - step),
        )

    def second_copy(k, step):
        return remote(
            second_send.at[k, step], second_recv.at[k, step - 1],
            r2_send.at[k, step - 1], r2_recv.at[k, step - 1], along_first(4 - step),
        )

    def step_pair(k):
        for t in range(WIDE // 128):
            pair_send[k, :, :, 128 * t : 128 * t + 128] = (
                partial[k, t, 256:512].astype(BF).reshape(16, 16, 128)
            )
        pair_copy(k).start()

    def step_first(k):
        pair_copy(k).wait_recv()
        for group in range(4):
            rows = slice(64 * group, 64 * group + 64)
            own_part = (lambda t, rows=rows: partial[k, t, rows], partial[k, 4, rows])
            span = slice(4 * group, 4 * group + 4)
            store_group(k, group, join([own_part, block_part(pair_recv, (k, span), 4)], spread))
        for step in (2, 1, 3):
            first_copy(k, step).start()

    def store_group(k, group, joined):
        tiles, top, total = joined
        tiles = tiles + [stat_tile(top, total)]
        for t in range(WIDE // 128):
            first_send[k, 4 * group : 4 * group + 4, :, 128 * t : 128 * t + 128] = (
                tiles[t].astype(BF).reshape(4, 16, 128)
            )

    def step_second(k):
        for step in range(1, 4):
            first_copy(k, step).wait_recv()
        parts = [block_part(first_send, (k, slice(0, 4)), 4)]
        parts += [block_part(first_recv, (k, step), 4) for step in range(3)]
        tiles, top, total = join(parts, spread)
        tiles = tiles + [stat_tile(top, total)]
        for t in range(WIDE // 128):
            second_send[k, :, :, 128 * t : 128 * t + 128] = tiles[t].astype(BF).reshape(4, 16, 128)
        for step in (2, 1, 3):
            second_copy(k, step).start()

    def step_last(k):
        for step in range(1, 4):
            second_copy(k, step).wait_recv()
        parts = [block_part(second_send, (k, 0), 1)]
        parts += [block_part(second_recv, (k, step), 1) for step in range(3)]
        tiles, _, total = join(parts, spread)
        for t in range(DC // 128):
            latent[16 * k : 16 * k + 16, 128 * t : 128 * t + 128] = (tiles[t] / total).astype(BF)

    cache_copy(0).wait()
    score(0, scores_a)
    soften(0, scores_a, probs_a, stats_a)

    def after(b, schedule):
        for when, step, k in schedule:
            pl.when(b == when)(functools.partial(step, k))

    def rollout_pair(i, carry):
        b = 2 * i
        cache_copy(b + 1).wait()
        cache_copy(b + 2).wait()
        score(b + 1, scores_b)
        weigh(b, probs_a, stats_a)
        soften(b + 1, scores_b, probs_b, stats_b)
        after(b, [(0, to_sibling, 1), (2, to_sibling, 2), (8, arrive, 2), (8, step_first, 0), (10, step_pair, 1)])
        score(b + 2, scores_a)
        weigh(b + 1, probs_b, stats_b)
        soften(b + 2, scores_a, probs_a, stats_a)
        after(b + 1, [(3, arrive, 1), (5, step_pair, 0), (13, step_first, 1)])
        return carry

    lax.fori_loop(0, B // 2 - 1, rollout_pair, 0)
    cache_copy(B - 1).wait()
    score(B - 1, scores_b)
    weigh(B - 2, probs_a, stats_a)
    soften(B - 1, scores_b, probs_b, stats_b)
    weigh(B - 1, probs_b, stats_b)
    step_pair(2)
    step_second(0)
    step_first(2)
    step_second(1)
    step_last(0)
    step_second(2)
    step_last(1)
    step_last(2)

    head_values = dot(latent[...], value_ref[...], NN).astype(BF)
    back = jnp.where(line == (column % S) * B + column // S, 1.0, 0.0).astype(BF)
    values[0] = dot(back, head_values, NN).astype(BF)

    def values_copy(peer):
        return remote(
            values.at[0], values.at[peer], v_send.at[peer - 1], v_recv.at[peer - 1], column_peer(peer)
        )

    for peer in range(1, 8):
        values_copy(peer).start()
    for peer in range(1, 8):
        weight_send(peer).wait_recv()
    for peer in range(1, 8):
        values_copy(peer).wait_recv()

    all_values = jnp.concatenate([values[peer] for peer in range(8)], axis=1)
    for strip in range(4):
        lanes = slice(256 * strip, 256 * strip + 256)
        features = dot(all_values, weights_all[:, :, lanes].reshape(8 * DN, 256), NN)
        for slot in range(4):
            piece = features[:, 64 * slot : 64 * slot + 64]
            out_send[4 * strip + slot] = jnp.concatenate(
                [
                    jnp.concatenate([piece[:16], piece[16:32]], axis=1),
                    jnp.concatenate([piece[32:], jnp.zeros((16, 64), F32)], axis=1),
                ],
                axis=0,
            ).astype(BF)

    def out_copy(peer):
        target = lax.rem(x + peer // 4, 4) * 4 + lax.rem(z + peer % 4, 4)
        return remote(
            out_send.at[target], out_recv.at[peer - 1],
            o_send.at[peer - 1], o_recv.at[peer - 1], plane_peer(peer),
        )

    for peer in (10, 2, 8, 6, 9, 11, 14, 1, 3, 4, 5, 7, 12, 13, 15):
        out_copy(peer).start()
    total = out_send[x * 4 + z].astype(F32)
    for peer in range(1, 16):
        out_copy(peer).wait_recv()
    for peer in range(1, 16):
        total = total + out_recv[peer - 1].astype(F32)
    out_ref[...] = jnp.concatenate(
        [total[:16, :FEAT], total[:16, 64 : 64 + FEAT], total[16:, :FEAT]], axis=0
    ).astype(BF)

    for k in range(CHUNKS):
        for step in range(1, 4):
            gather_one(k, step).wait_send()
            first_copy(k, step).wait_send()
            second_copy(k, step).wait_send()
            gather_two(k, step).wait_send()
        for group in range(4):
            gather_three(k, group).wait_send()
        pair_copy(k).wait_send()
    for peer in range(1, 8):
        weight_send(peer).wait_send()
        values_copy(peer).wait_send()
    for peer in range(1, 16):
        out_copy(peer).wait_send()


def body(query_heads, key_up, value_up, output_weight, latent_cache, lengths, positions):
    query = jnp.transpose(query_heads[:, :, 0, :], (1, 0, 2)).reshape(ROWS, DN + DR)
    cache = jnp.swapaxes(latent_cache, 1, 2)
    width = output_weight.shape[1]
    dma = pltpu.SemaphoreType.DMA
    vmem, smem = pltpu.VMEM, pltpu.SMEM
    out = pl.pallas_call(
        kernel,
        out_shape=jax.ShapeDtypeStruct((ROWS, FEAT), BF),
        in_specs=[
            pl.BlockSpec(memory_space=smem),
            pl.BlockSpec(memory_space=smem),
            pl.BlockSpec(memory_space=vmem),
            pl.BlockSpec(memory_space=vmem),
            pl.BlockSpec(memory_space=vmem),
            pl.BlockSpec(memory_space=pl.ANY),
            pl.BlockSpec(memory_space=pl.ANY),
        ],
        out_specs=pl.BlockSpec(memory_space=vmem),
        scratch_shapes=[
            vmem((B, RANK, SHARD), BF),
            vmem((DN, width), BF),
            vmem((2, 4, DN, 1024), BF),
            vmem((8, DN, 1024), BF),
            vmem((2, CHUNKS, 16, 16, WIDE), BF),
            vmem((CHUNKS, WIDE // 128, 512, 128), F32),
            vmem((96, SHARD), F32),
            vmem((96, SHARD), F32),
            vmem((96, SHARD), BF),
            vmem((96, SHARD), BF),
            vmem((96, 128), F32),
            vmem((96, 128), F32),
            vmem((CHUNKS, WIDE // 128, 512, 128), F32),
            vmem((CHUNKS, 16, 16, WIDE), BF),
            vmem((CHUNKS, 16, 16, WIDE), BF),
            vmem((CHUNKS, 16, 16, WIDE), BF),
            vmem((CHUNKS, 3, 4, 16, WIDE), BF),
            vmem((CHUNKS, 4, 16, WIDE), BF),
            vmem((CHUNKS, 3, 16, WIDE), BF),
            vmem((ROWS, DC), BF),
            vmem((8, ROWS, 128), BF),
            vmem((16, 32, 128), BF),
            vmem((15, 32, 128), BF),
            vmem((128, 256), BF),
            dma((B,)),
            dma((1,)),
            dma((CHUNKS, 3)), dma((CHUNKS, 3)),
            dma((CHUNKS, 3)), dma((CHUNKS, 3)),
            dma((CHUNKS, 4)), dma((CHUNKS, 4)),
            dma((CHUNKS,)), dma((CHUNKS,)),
            dma((CHUNKS, 3)), dma((CHUNKS, 3)),
            dma((CHUNKS, 3)), dma((CHUNKS, 3)),
            dma((7,)), dma((7,)),
            dma((7,)), dma((7,)),
            dma((15,)), dma((15,)),
        ],
        compiler_params=pltpu.CompilerParams(
            collective_id=0, has_side_effects=True, vmem_limit_bytes=56 * 2**20
        ),
    )(lengths, positions, query, key_up[0], value_up[0], output_weight, cache)
    return jnp.transpose(out.reshape(S, B, FEAT), (1, 0, 2))


def solution(mesh):
    in_specs = (
        P(None, None, ("kv", "head"), None),
        P(("kv", "head"), None, None),
        P(("kv", "head"), None, None),
        P(("kv", "head"), None),
        P(None, "kv", None),
        P(),
        P(),
    )
    out_specs = P(None, None, ("kv", "head"))
    return jax.shard_map(body, mesh=mesh, in_specs=in_specs, out_specs=out_specs, check_vma=False)
```

```python
import functools

import jax
import jax.numpy as jnp
import numpy as np
from jax import lax
from jax.experimental import pallas as pl
from jax.experimental.pallas import tpu as pltpu
from jax.sharding import PartitionSpec as P

MESH = pl.DeviceIdType.MESH
BF = jnp.bfloat16
F32 = jnp.float32

DN = 128
DR = 64
DC = 512
B = 16
S = 3
ROWS = B * S
CHUNKS = ROWS // 16
RANK = DC + DR
WIDE = 640
SHARD = 1024
FEAT = 56
MASKED = -(2.0**100)
PLANE_ORDER = (10, 6, 9, 11, 14, 2, 8, 5, 7, 13, 15, 1, 3, 4, 12)
FACTOR = float(np.log2(np.e) / np.sqrt(DN + DR))

dot = functools.partial(lax.dot_general, preferred_element_type=F32)
NN = (((1,), (0,)), ((), ()))
NT = (((1,), (1,)), ((), ()))


def split3(value):
    high = value.astype(BF).astype(F32)
    rest = value - high
    middle = rest.astype(BF).astype(F32)
    return high, middle, rest - middle


def stat_tile(top, total):
    lane = lax.broadcasted_iota(jnp.int32, (top.shape[0], 128), 1)
    top_high, top_middle, top_low = split3(top)
    total_high, total_middle, _ = split3(total)
    tile = jnp.where(lane == 4, total_middle, 0.0)
    tile = jnp.where(lane == 3, total_high, tile)
    tile = jnp.where(lane == 2, top_low, tile)
    tile = jnp.where(lane == 1, top_middle, tile)
    return jnp.where(lane == 0, top_high, tile)


def spread_matrix():
    source = lax.broadcasted_iota(jnp.int32, (128, 256), 0)
    target = lax.broadcasted_iota(jnp.int32, (128, 256), 1)
    is_top = (source < 3) & (target < 128)
    is_total = (source >= 3) & (source < 5) & (target >= 128)
    return jnp.where(is_top | is_total, 1.0, 0.0).astype(BF)


def spread_stats(tile, spread):
    both = dot(tile.astype(BF), spread[...], NN)
    return both[:, :128], both[:, 128:]


def join(parts, spread):
    stats = [spread_stats(tile, spread) for _, tile in parts]
    top = functools.reduce(jnp.maximum, [m for m, _ in stats])
    factors = [jnp.exp2((m - top) * FACTOR) for m, _ in stats]
    total = sum(f * l for f, (_, l) in zip(factors, stats))
    tiles = []
    for t in range(DC // 128):
        tiles.append(sum(f * data(t) for f, (data, _) in zip(factors, parts)))
    return tiles, top, total


def join_stack(ref, spread):
    count = ref.shape[0]
    tops, totals = spread_stats(ref[:, :, DC:].reshape(count * 16, 128), spread)
    tops = tops.reshape(count, 16, 128)
    top = jnp.max(tops, axis=0)
    factors = jnp.exp2((tops - top[None]) * FACTOR)
    total = jnp.sum(factors * totals.reshape(count, 16, 128), axis=0)
    tiles = [
        jnp.sum(factors * ref[:, :, 128 * t : 128 * t + 128].astype(F32), axis=0)
        for t in range(DC // 128)
    ]
    return tiles, top, total


def block_part(ref, index, count):
    rows = count * 16

    def data(t):
        return ref[index][..., 128 * t : 128 * t + 128].astype(F32).reshape(rows, 128)

    return data, ref[index][..., DC:WIDE].reshape(rows, 128)


def kernel(
    lengths_hbm, positions_hbm, query_hbm, key_hbm, value_hbm, weight_hbm, cache_hbm, out_ref,
    lengths_ref, positions_ref, query_ref, key_ref, value_ref,
    cache, weight, wide, weights_all, gathered, query_f32, scores_a, scores_b, probs_a, probs_b,
    stats_a, stats_b, partial, pair_send, pair_recv, first_send, first_recv, second_send, second_recv,
    latent, values, out_send, out_recv,
    last_recv, spread, cache_sem, small_sem, g1_send, g1_recv, g2_send, g2_recv, g3_send, g3_recv,
    pair_ss, pair_rs, r1_send, r1_recv, r2_send, r2_recv, w_send, w_recv, v_send, v_recv, o_send, o_recv,
):
    kv = lax.axis_index("kv")
    row_y = lax.axis_index("head")
    x, z, core = kv // 8, (kv // 2) % 4, kv % 2

    def place(px, pz, pc, py):
        return (lax.rem(px, 4) * 8 + lax.rem(pz, 4) * 2 + pc, lax.rem(py, 4))

    def along_first(step):
        return plane_peer(step)

    def along_second(step):
        return plane_peer(4 * step)

    def column_peer(peer):
        return place(x, z, lax.rem(core + peer // 4, 2), row_y + peer % 4)

    def plane_peer(peer):
        first, second = peer % 4, peer // 4
        return place(
            x + first * (1 - core) + second * core, z + second * (1 - core) + first * core, core, row_y
        )

    sibling = place(x, z, 1 - core, row_y)

    def remote(src, dst, send, recv, device):
        return pltpu.make_async_remote_copy(
            src_ref=src, dst_ref=dst, send_sem=send, recv_sem=recv,
            device_id=device, device_id_type=MESH,
        )

    def arrived(ref, semaphore):
        remote(ref, ref, semaphore, semaphore, sibling).wait_recv()

    def departed(ref, semaphore):
        remote(ref, ref, semaphore, semaphore, sibling).wait_send()

    def cache_copy(pair):
        span = pl.ds(2 * pair, 2)
        return pltpu.make_async_copy(cache_hbm.at[span], cache.at[span], cache_sem.at[pair])

    small_copies = [
        pltpu.make_async_copy(source, target, small_sem.at[i])
        for i, (source, target) in enumerate([
            (positions_hbm, positions_ref), (query_hbm, query_ref), (key_hbm, key_ref),
            (lengths_hbm, lengths_ref), (weight_hbm, weight), (value_hbm, value_ref),
        ])
    ]

    barrier = pltpu.get_barrier_semaphore()
    partners = [plane_peer(peer) for peer in PLANE_ORDER] + [column_peer(peer) for peer in range(1, 8)]
    for partner in partners:
        pl.semaphore_signal(barrier, inc=1, device_id=partner, device_id_type=MESH)
    for copy in small_copies:
        copy.start()
    for pair in range(B // 2):
        cache_copy(pair).start()

    spread[...] = spread_matrix()

    for copy in small_copies[:4]:
        copy.wait()
    line = lax.broadcasted_iota(jnp.int32, (ROWS, ROWS), 0)
    column = lax.broadcasted_iota(jnp.int32, (ROWS, ROWS), 1)
    reorder = jnp.where(column == (line % S) * B + line // S, 1.0, 0.0).astype(BF)
    query = dot(reorder, query_ref[...], NN)
    query_latent = dot(query[:, :DN].astype(BF), key_ref[...], NN)
    lane = lax.broadcasted_iota(jnp.int32, (ROWS, DR // 2), 1).astype(F32)
    frequency = jnp.exp(lane * (-np.log(10000.0) / (DR // 2)))
    token_row = lax.broadcasted_iota(jnp.int32, (ROWS, DR // 2), 0)
    spot = jnp.zeros((ROWS, DR // 2), jnp.int32)
    for b in range(B):
        spot = jnp.where(token_row // S == b, positions_ref[b], spot)
    angle = (spot + token_row % S).astype(F32) * frequency
    cosine, sine = jnp.cos(angle), jnp.sin(angle)
    first_half, second_half = query[:, DN : DN + DR // 2], query[:, DN + DR // 2 :]
    own = jnp.concatenate(
        [
            query_latent,
            first_half * cosine - second_half * sine,
            second_half * cosine + first_half * sine,
            jnp.zeros((ROWS, WIDE - RANK), F32),
        ],
        axis=1,
    ).astype(BF)
    for k in range(CHUNKS):
        gathered[0, k, 0] = own[16 * k : 16 * k + 16]

    pl.semaphore_wait(barrier, len(partners))

    def gather_one(k, peer):
        return remote(
            gathered.at[0, k, 0], gathered.at[0, k, peer], g1_send.at[k],
            g1_recv.at[CHUNKS if k == 0 and peer >= 8 else k], plane_peer(peer),
        )

    def gather_two(k, step):
        return remote(
            gathered.at[0, k, pl.ds(0, 4)], gathered.at[0, k, pl.ds(4 * step, 4)],
            g2_send.at[k], g2_recv.at[k], along_second(step),
        )

    def gather_three(k, start, count):
        span = pl.ds(start, count)
        return remote(
            gathered.at[0, k, span], gathered.at[1, k, span], g3_send.at[k], g3_recv.at[k], sibling
        )

    for peer in (2, 5, 6, 7, 1, 3, 4, 10, 8, 9, 11, 14, 13, 15, 12):
        gather_one(0, peer).start()
    for k in range(1, CHUNKS):
        for step in (2, 1, 3):
            gather_one(k, step).start()

    small_copies[4].wait()

    def widen(g, carry):
        base = pl.multiple_of(g * (16 * FEAT), 128)
        strip = weight[:, pl.ds(base, 16 * FEAT)]
        gap = jnp.zeros((DN, 64 - FEAT), BF)
        for parity in range(2):
            for side in range(4):
                start = (parity * 4 + side) * FEAT
                wide[parity, side, :, pl.ds(pl.multiple_of(g * 128, 128), 128)] = jnp.concatenate(
                    [strip[:, start : start + FEAT], gap,
                     strip[:, start + 8 * FEAT : start + 9 * FEAT], gap], axis=1)
        return carry

    lax.fori_loop(0, 8, widen, 0)

    def weight_send(peer):
        turn, step = peer // 4, peer % 4
        return remote(
            wide.at[lax.rem(core + turn, 2), lax.rem(row_y + step, 4)], weights_all.at[peer],
            w_send.at[0], w_recv.at[0], column_peer(peer),
        )

    for peer in range(1, 8):
        weight_send(peer).start()
    weights_all[0] = wide[core, row_y]

    def to_second(k):
        arrived(gathered.at[0, k, pl.ds(1, 3)], g1_recv.at[k])
        for step in (2, 1, 3):
            gather_two(k, step).start()
        gather_three(k, 0, 4).start()

    def to_sibling(k):
        arrived(gathered.at[0, k, pl.ds(4, 12)], g2_recv.at[k])
        gather_three(k, 4, 12).start()

    def unpack(k):
        for parity in range(2):
            for t in range(WIDE // 128):
                query_f32[k, t, parity * 256 : parity * 256 + 256] = (
                    gathered[parity, k, :, :, 128 * t : 128 * t + 128].astype(F32).reshape(256, 128)
                )

    def arrive(k):
        arrived(gathered.at[1, k], g3_recv.at[k])
        unpack(k)

    arrived(gathered.at[0, 0, pl.ds(1, 7)], g1_recv.at[0])
    gather_three(0, 0, 8).start()
    arrived(gathered.at[0, 0, pl.ds(8, 8)], g1_recv.at[CHUNKS])
    gather_three(0, 8, 8).start()
    to_second(1)
    to_second(2)
    arrive(0)

    slots = lax.broadcasted_iota(jnp.int32, (1, SHARD), 1)

    def score(b, target):
        rows = []
        for s in range(S):
            r = b * S + s
            tiles = [
                query_f32[r // 16, t, pl.ds(r % 16, 32, stride=16), :] for t in range(WIDE // 128)
            ]
            rows.append(jnp.concatenate(tiles, axis=1)[:, :RANK])
        target[...] = dot(jnp.concatenate(rows, axis=0).astype(BF), cache[b], NN)

    def soften(b, source, target, stats):
        for s in range(S):
            last = lengths_ref[b] - S + s - kv * SHARD
            part = jnp.where(slots <= last, source[32 * s : 32 * s + 32, :], MASKED)
            top = jnp.max(part, axis=1, keepdims=True)
            weights = jnp.exp2((part - top) * FACTOR)
            total = jnp.sum(weights, axis=1, keepdims=True)
            target[32 * s : 32 * s + 32, :] = weights.astype(BF)
            stats[32 * s : 32 * s + 32, :] = stat_tile(top, total)

    def weigh(b, source, stats):
        numerators = dot(source[...], cache[b, :DC], NT)
        for s in range(S):
            r = b * S + s
            for t in range(DC // 128):
                partial[r // 16, t, pl.ds(r % 16, 32, stride=16), :] = numerators[
                    32 * s : 32 * s + 32, 128 * t : 128 * t + 128
                ]
            partial[r // 16, 4, pl.ds(r % 16, 32, stride=16), :] = stats[32 * s : 32 * s + 32, :]

    def pair_copy(k):
        return remote(pair_send.at[k], pair_recv.at[k], pair_ss.at[k], pair_rs.at[k], sibling)

    def first_copy(k, step):
        return remote(
            first_send.at[k, pl.ds(4 * step, 4)], first_recv.at[k, step - 1],
            r1_send.at[k], r1_recv.at[k], along_second(4 - step),
        )

    def second_copy(k, step):
        return remote(
            second_send.at[k, step], second_recv.at[k, step - 1],
            r2_send.at[k], r2_recv.at[k], along_first(4 - step),
        )

    def step_pair(k):
        for t in range(WIDE // 128):
            pair_send[k, :, :, 128 * t : 128 * t + 128] = (
                partial[k, t, 256:512].astype(BF).reshape(16, 16, 128)
            )
        pair_copy(k).start()

    def step_first(k):
        pair_copy(k).wait_recv()
        for group in range(4):
            rows = slice(64 * group, 64 * group + 64)
            own_part = (lambda t, rows=rows: partial[k, t, rows], partial[k, 4, rows])
            span = slice(4 * group, 4 * group + 4)
            store_group(k, group, join([own_part, block_part(pair_recv, (k, span), 4)], spread))
        if k < CHUNKS - 1:
            for step in (2, 1, 3):
                first_copy(k, step).start()
        else:
            for peer in PLANE_ORDER:
                last_copy(peer).start()
            last_recv[0] = first_send[k, 0]

    def last_copy(peer):
        back = (4 - peer // 4) % 4 * 4 + (4 - peer % 4) % 4
        return remote(
            first_send.at[CHUNKS - 1, peer], last_recv.at[peer],
            r1_send.at[CHUNKS - 1], r1_recv.at[CHUNKS - 1], plane_peer(back),
        )

    def store_group(k, group, joined):
        tiles, top, total = joined
        tiles = tiles + [stat_tile(top, total)]
        for t in range(WIDE // 128):
            first_send[k, 4 * group : 4 * group + 4, :, 128 * t : 128 * t + 128] = (
                tiles[t].astype(BF).reshape(4, 16, 128)
            )

    def step_second(k):
        arrived(first_recv.at[k], r1_recv.at[k])
        parts = [block_part(first_send, (k, slice(0, 4)), 4)]
        parts += [block_part(first_recv, (k, step), 4) for step in range(3)]
        tiles, top, total = join(parts, spread)
        tiles = tiles + [stat_tile(top, total)]
        for t in range(WIDE // 128):
            second_send[k, :, :, 128 * t : 128 * t + 128] = tiles[t].astype(BF).reshape(4, 16, 128)
        for step in (2, 1, 3):
            second_copy(k, step).start()

    def step_last(k):
        if k < CHUNKS - 1:
            arrived(second_recv.at[k], r2_recv.at[k])
            parts = [block_part(second_send, (k, 0), 1)]
            parts += [block_part(second_recv, (k, step), 1) for step in range(3)]
            tiles, _, total = join(parts, spread)
        else:
            arrived(last_recv.at[pl.ds(1, 15)], r1_recv.at[k])
            tiles, _, total = join_stack(last_recv, spread)
        for t in range(DC // 128):
            latent[16 * k : 16 * k + 16, 128 * t : 128 * t + 128] = (tiles[t] / total).astype(BF)

    cache_copy(0).wait()
    score(0, scores_a)
    soften(0, scores_a, probs_a, stats_a)

    def after(b, schedule):
        for when, step, k in schedule:
            pl.when(b == when)(functools.partial(step, k))

    def rollout_pair(i, carry):
        b = 2 * i
        cache_copy(i + 1).wait()
        score(b + 1, scores_b)
        weigh(b, probs_a, stats_a)
        soften(b + 1, scores_b, probs_b, stats_b)
        after(b, [(0, to_sibling, 1), (2, to_sibling, 2), (8, arrive, 2), (8, step_first, 0), (10, step_pair, 1)])
        score(b + 2, scores_a)
        weigh(b + 1, probs_b, stats_b)
        soften(b + 2, scores_a, probs_a, stats_a)
        after(b + 1, [(3, arrive, 1), (5, step_pair, 0), (13, step_first, 1)])
        return carry

    lax.fori_loop(0, B // 2 - 1, rollout_pair, 0)
    score(B - 1, scores_b)
    weigh(B - 2, probs_a, stats_a)
    soften(B - 1, scores_b, probs_b, stats_b)
    weigh(B - 1, probs_b, stats_b)
    step_pair(2)
    step_second(0)
    step_first(2)
    step_second(1)
    step_last(0)
    step_last(1)
    step_last(2)

    small_copies[5].wait()

    head_values = dot(latent[...], value_ref[...], NN).astype(BF)
    back = jnp.where(line == (column % S) * B + column // S, 1.0, 0.0).astype(BF)
    values[0] = dot(back, head_values, NN).astype(BF)

    def values_copy(peer):
        return remote(
            values.at[0], values.at[peer], v_send.at[0], v_recv.at[0], column_peer(peer)
        )

    for peer in range(1, 8):
        values_copy(peer).start()
    arrived(weights_all.at[pl.ds(1, 7)], w_recv.at[0])
    arrived(values.at[pl.ds(1, 7)], v_recv.at[0])

    all_values = jnp.concatenate([values[peer] for peer in range(8)], axis=1)
    for strip in range(4):
        lanes = slice(256 * strip, 256 * strip + 256)
        features = dot(all_values, weights_all[:, :, lanes].reshape(8 * DN, 256), NN)
        for slot in range(4):
            piece = features[:, 64 * slot : 64 * slot + 64]
            out_send[4 * strip + slot] = jnp.concatenate(
                [
                    jnp.concatenate([piece[:16], piece[16:32]], axis=1),
                    jnp.concatenate([piece[32:], jnp.zeros((16, 64), F32)], axis=1),
                ],
                axis=0,
            ).astype(BF)

    def out_copy(peer):
        first, second = peer % 4, peer // 4
        target = lax.rem(x + first * (1 - core) + second * core, 4) * 4 + lax.rem(
            z + second * (1 - core) + first * core, 4
        )
        return remote(
            out_send.at[target], out_recv.at[peer - 1],
            o_send.at[0], o_recv.at[0], plane_peer(peer),
        )

    for peer in PLANE_ORDER:
        out_copy(peer).start()
    total = out_send[x * 4 + z].astype(F32)
    arrived(out_recv, o_recv.at[0])
    for peer in range(1, 16):
        total = total + out_recv[peer - 1].astype(F32)
    out_ref[...] = jnp.concatenate(
        [total[:16, :FEAT], total[:16, 64 : 64 + FEAT], total[16:, :FEAT]], axis=0
    ).astype(BF)

    for k in range(CHUNKS):
        departed(gathered.at[0, k, pl.ds(1, 15 if k == 0 else 3)], g1_send.at[k])
        departed(gathered.at[0, k], g3_send.at[k])
        departed(pair_recv.at[k], pair_ss.at[k])
        if k > 0:
            departed(gathered.at[0, k, pl.ds(4, 12)], g2_send.at[k])
        if k < CHUNKS - 1:
            departed(first_recv.at[k], r1_send.at[k])
            departed(second_recv.at[k], r2_send.at[k])
        else:
            departed(last_recv.at[pl.ds(1, 15)], r1_send.at[k])
    departed(weights_all.at[pl.ds(1, 7)], w_send.at[0])
    departed(values.at[pl.ds(1, 7)], v_send.at[0])
    departed(out_recv, o_send.at[0])


def body(query_heads, key_up, value_up, output_weight, latent_cache, lengths, positions):
    query = jnp.transpose(query_heads[:, :, 0, :], (1, 0, 2)).reshape(ROWS, DN + DR)
    cache = jnp.swapaxes(latent_cache, 1, 2)
    width = output_weight.shape[1]
    dma = pltpu.SemaphoreType.DMA
    vmem, smem = pltpu.VMEM, pltpu.SMEM
    out = pl.pallas_call(
        kernel,
        out_shape=jax.ShapeDtypeStruct((ROWS, FEAT), BF),
        in_specs=[
            pl.BlockSpec(memory_space=pl.ANY) for _ in range(7)
        ],
        out_specs=pl.BlockSpec(memory_space=vmem),
        scratch_shapes=[
            smem((B,), jnp.int32),
            smem((B,), jnp.int32),
            vmem((ROWS, DN + DR), BF),
            vmem((DN, DC), BF),
            vmem((DC, 128), BF),
            vmem((B, RANK, SHARD), BF),
            vmem((DN, width), BF),
            vmem((2, 4, DN, 1024), BF),
            vmem((8, DN, 1024), BF),
            vmem((2, CHUNKS, 16, 16, WIDE), BF),
            vmem((CHUNKS, WIDE // 128, 512, 128), F32),
            vmem((96, SHARD), F32),
            vmem((96, SHARD), F32),
            vmem((96, SHARD), BF),
            vmem((96, SHARD), BF),
            vmem((96, 128), F32),
            vmem((96, 128), F32),
            vmem((CHUNKS, WIDE // 128, 512, 128), F32),
            vmem((CHUNKS, 16, 16, WIDE), BF),
            vmem((CHUNKS, 16, 16, WIDE), BF),
            vmem((CHUNKS, 16, 16, WIDE), BF),
            vmem((CHUNKS, 3, 4, 16, WIDE), BF),
            vmem((CHUNKS, 4, 16, WIDE), BF),
            vmem((CHUNKS, 3, 16, WIDE), BF),
            vmem((ROWS, DC), BF),
            vmem((8, ROWS, 128), BF),
            vmem((16, 32, 128), BF),
            vmem((15, 32, 128), BF),
            vmem((16, 16, WIDE), BF),
            vmem((128, 256), BF),
            dma((B // 2,)),
            dma((6,)),
            dma((CHUNKS,)), dma((CHUNKS + 1,)),
            dma((CHUNKS,)), dma((CHUNKS,)),
            dma((CHUNKS,)), dma((CHUNKS,)),
            dma((CHUNKS,)), dma((CHUNKS,)),
            dma((CHUNKS,)), dma((CHUNKS,)),
            dma((CHUNKS,)), dma((CHUNKS,)),
            dma((1,)), dma((1,)),
            dma((1,)), dma((1,)),
            dma((1,)), dma((1,)),
        ],
        compiler_params=pltpu.CompilerParams(
            collective_id=0, has_side_effects=True, vmem_limit_bytes=56 * 2**20
        ),
    )(lengths, positions, query, key_up[0], value_up[0], output_weight, cache)
    return jnp.transpose(out.reshape(S, B, FEAT), (1, 0, 2))


def solution(mesh):
    in_specs = (
        P(None, None, ("kv", "head"), None),
        P(("kv", "head"), None, None),
        P(("kv", "head"), None, None),
        P(("kv", "head"), None),
        P(None, "kv", None),
        P(),
        P(),
    )
    out_specs = P(None, None, ("kv", "head"))
    return jax.shard_map(body, mesh=mesh, in_specs=in_specs, out_specs=out_specs, check_vma=False)
```

```python
import functools

import jax
import jax.numpy as jnp
import numpy as np
from jax import lax
from jax.experimental import pallas as pl
from jax.experimental.pallas import tpu as pltpu
from jax.sharding import PartitionSpec as P

MESH = pl.DeviceIdType.MESH
BF = jnp.bfloat16
F32 = jnp.float32

DN = 128
DR = 64
DC = 512
B = 16
S = 3
ROWS = B * S
CHUNKS = ROWS // 16
RANK = DC + DR
WIDE = 640
SHARD = 1024
FEAT = 56
MASKED = -(2.0**100)
PLANE_ORDER = (10, 6, 9, 11, 14, 2, 8, 5, 7, 13, 15, 1, 3, 4, 12)
FACTOR = float(np.log2(np.e) / np.sqrt(DN + DR))

dot = functools.partial(lax.dot_general, preferred_element_type=F32)
NN = (((1,), (0,)), ((), ()))
NT = (((1,), (1,)), ((), ()))


def split3(value):
    high = value.astype(BF).astype(F32)
    rest = value - high
    middle = rest.astype(BF).astype(F32)
    return high, middle, rest - middle


def stat_tile(top, total):
    lane = lax.broadcasted_iota(jnp.int32, (top.shape[0], 128), 1)
    top_high, top_middle, top_low = split3(top)
    total_high, total_middle, _ = split3(total)
    tile = jnp.where(lane == 4, total_middle, 0.0)
    tile = jnp.where(lane == 3, total_high, tile)
    tile = jnp.where(lane == 2, top_low, tile)
    tile = jnp.where(lane == 1, top_middle, tile)
    return jnp.where(lane == 0, top_high, tile)


def spread_matrix():
    source = lax.broadcasted_iota(jnp.int32, (128, 256), 0)
    target = lax.broadcasted_iota(jnp.int32, (128, 256), 1)
    is_top = (source < 3) & (target < 128)
    is_total = (source >= 3) & (source < 5) & (target >= 128)
    return jnp.where(is_top | is_total, 1.0, 0.0).astype(BF)


def spread_stats(tile, spread):
    both = dot(tile.astype(BF), spread[...], NN)
    return both[:, :128], both[:, 128:]


def join(parts, spread):
    stats = [spread_stats(tile, spread) for _, tile in parts]
    top = functools.reduce(jnp.maximum, [m for m, _ in stats])
    factors = [jnp.exp2((m - top) * FACTOR) for m, _ in stats]
    total = sum(f * l for f, (_, l) in zip(factors, stats))
    tiles = []
    for t in range(DC // 128):
        tiles.append(sum(f * data(t) for f, (data, _) in zip(factors, parts)))
    return tiles, top, total


def join_stack(ref, spread):
    count = ref.shape[0]
    tops, totals = spread_stats(ref[:, :, DC:].reshape(count * 16, 128), spread)
    tops = tops.reshape(count, 16, 128)
    top = jnp.max(tops, axis=0)
    factors = jnp.exp2((tops - top[None]) * FACTOR)
    total = jnp.sum(factors * totals.reshape(count, 16, 128), axis=0)
    tiles = [
        jnp.sum(factors * ref[:, :, 128 * t : 128 * t + 128].astype(F32), axis=0)
        for t in range(DC // 128)
    ]
    return tiles, top, total


def block_part(ref, index, count):
    rows = count * 16

    def data(t):
        return ref[index][..., 128 * t : 128 * t + 128].astype(F32).reshape(rows, 128)

    return data, ref[index][..., DC:WIDE].reshape(rows, 128)


def kernel(
    lengths_hbm, positions_hbm, query_hbm, key_hbm, value_hbm, weight_hbm, cache_hbm, out_ref,
    lengths_ref, positions_ref, query_ref, key_ref, value_ref,
    cache, weight, wide, weights_all, gathered, query_f32, scores_a, scores_b, probs_a, probs_b,
    stats_a, stats_b, partial, pair_send, pair_recv, first_send, first_recv, second_send, second_recv,
    latent, values, out_send, out_recv,
    last_recv, spread, cache_sem, small_sem, g1_send, g1_recv, g2_send, g2_recv, g3_send, g3_recv,
    pair_ss, pair_rs, r1_send, r1_recv, r2_send, r2_recv, w_send, w_recv, v_send, v_recv, o_send, o_recv,
):
    kv = lax.axis_index("kv")
    row_y = lax.axis_index("head")
    x, z, core = kv // 8, (kv // 2) % 4, kv % 2

    def place(px, pz, pc, py):
        return (lax.rem(px, 4) * 8 + lax.rem(pz, 4) * 2 + pc, lax.rem(py, 4))

    def along_first(step):
        return plane_peer(step)

    def along_second(step):
        return plane_peer(4 * step)

    def column_peer(peer):
        return place(x, z, lax.rem(core + peer // 4, 2), row_y + peer % 4)

    def plane_peer(peer):
        first, second = peer % 4, peer // 4
        return place(
            x + first * (1 - core) + second * core, z + second * (1 - core) + first * core, core, row_y
        )

    sibling = place(x, z, 1 - core, row_y)

    def remote(src, dst, send, recv, device):
        return pltpu.make_async_remote_copy(
            src_ref=src, dst_ref=dst, send_sem=send, recv_sem=recv,
            device_id=device, device_id_type=MESH,
        )

    def arrived(ref, semaphore):
        remote(ref, ref, semaphore, semaphore, sibling).wait_recv()

    def departed(ref, semaphore):
        remote(ref, ref, semaphore, semaphore, sibling).wait_send()

    def cache_copy(pair):
        span = pl.ds(2 * pair, 2)
        return pltpu.make_async_copy(cache_hbm.at[span], cache.at[span], cache_sem.at[pair])

    small_copies = [
        pltpu.make_async_copy(source, target, small_sem.at[i])
        for i, (source, target) in enumerate([
            (positions_hbm, positions_ref), (query_hbm, query_ref), (key_hbm, key_ref),
            (lengths_hbm, lengths_ref), (weight_hbm, weight), (value_hbm, value_ref),
        ])
    ]

    barrier = pltpu.get_barrier_semaphore()
    partners = [plane_peer(peer) for peer in PLANE_ORDER] + [column_peer(peer) for peer in range(1, 8)]
    for partner in partners:
        pl.semaphore_signal(barrier, inc=1, device_id=partner, device_id_type=MESH)
    for copy in small_copies:
        copy.start()
    for pair in range(B // 2):
        cache_copy(pair).start()

    spread[...] = spread_matrix()

    for copy in small_copies[:4]:
        copy.wait()
    line = lax.broadcasted_iota(jnp.int32, (ROWS, ROWS), 0)
    column = lax.broadcasted_iota(jnp.int32, (ROWS, ROWS), 1)
    reorder = jnp.where(column == (line % S) * B + line // S, 1.0, 0.0).astype(BF)
    query = dot(reorder, query_ref[...], NN)
    query_latent = dot(query[:, :DN].astype(BF), key_ref[...], NN)
    lane = lax.broadcasted_iota(jnp.int32, (ROWS, DR // 2), 1).astype(F32)
    frequency = jnp.exp(lane * (-np.log(10000.0) / (DR // 2)))
    token_row = lax.broadcasted_iota(jnp.int32, (ROWS, DR // 2), 0)
    spot = jnp.zeros((ROWS, DR // 2), jnp.int32)
    for b in range(B):
        spot = jnp.where(token_row // S == b, positions_ref[b], spot)
    angle = (spot + token_row % S).astype(F32) * frequency
    cosine, sine = jnp.cos(angle), jnp.sin(angle)
    first_half, second_half = query[:, DN : DN + DR // 2], query[:, DN + DR // 2 :]
    own = jnp.concatenate(
        [
            query_latent,
            first_half * cosine - second_half * sine,
            second_half * cosine + first_half * sine,
            jnp.zeros((ROWS, WIDE - RANK), F32),
        ],
        axis=1,
    ).astype(BF)
    for k in range(CHUNKS):
        gathered[0, k, 0] = own[16 * k : 16 * k + 16]

    pl.semaphore_wait(barrier, len(partners))

    def gather_one(k, peer):
        return remote(
            gathered.at[0, k, 0], gathered.at[0, k, peer], g1_send.at[k],
            g1_recv.at[CHUNKS if k == 0 and peer >= 8 else k], plane_peer(peer),
        )

    def gather_two(k, step):
        return remote(
            gathered.at[0, k, pl.ds(0, 4)], gathered.at[0, k, pl.ds(4 * step, 4)],
            g2_send.at[k], g2_recv.at[k], along_second(step),
        )

    def gather_three(k, start, count):
        span = pl.ds(start, count)
        return remote(
            gathered.at[0, k, span], gathered.at[1, k, span], g3_send.at[k], g3_recv.at[k], sibling
        )

    for step in (2, 1, 3):
        gather_one(1, step).start()
    for peer in (2, 5, 6, 7, 1, 3, 4, 10, 8, 9, 11, 14, 13, 15, 12):
        gather_one(0, peer).start()
    for step in (2, 1, 3):
        gather_one(2, step).start()

    small_copies[4].wait()

    def widen(g, carry):
        base = pl.multiple_of(g * (16 * FEAT), 128)
        strip = weight[:, pl.ds(base, 16 * FEAT)]
        gap = jnp.zeros((DN, 64 - FEAT), BF)
        for parity in range(2):
            for side in range(4):
                start = (parity * 4 + side) * FEAT
                wide[parity, side, :, pl.ds(pl.multiple_of(g * 128, 128), 128)] = jnp.concatenate(
                    [strip[:, start : start + FEAT], gap,
                     strip[:, start + 8 * FEAT : start + 9 * FEAT], gap], axis=1)
        return carry

    lax.fori_loop(0, 8, widen, 0)

    def weight_send(peer):
        turn, step = peer // 4, peer % 4
        return remote(
            wide.at[lax.rem(core + turn, 2), lax.rem(row_y + step, 4)], weights_all.at[peer],
            w_send.at[0], w_recv.at[0], column_peer(peer),
        )

    for peer in range(1, 8):
        weight_send(peer).start()
    weights_all[0] = wide[core, row_y]

    def to_second(k):
        arrived(gathered.at[0, k, pl.ds(1, 3)], g1_recv.at[k])
        for step in (2, 1, 3):
            gather_two(k, step).start()
        gather_three(k, 0, 4).start()

    def to_sibling(k):
        arrived(gathered.at[0, k, pl.ds(4, 12)], g2_recv.at[k])
        gather_three(k, 4, 12).start()

    def unpack(k):
        for parity in range(2):
            for t in range(WIDE // 128):
                query_f32[k, t, parity * 256 : parity * 256 + 256] = (
                    gathered[parity, k, :, :, 128 * t : 128 * t + 128].astype(F32).reshape(256, 128)
                )

    def arrive(k):
        arrived(gathered.at[1, k], g3_recv.at[k])
        unpack(k)

    to_second(1)
    arrived(gathered.at[0, 0, pl.ds(1, 7)], g1_recv.at[0])
    gather_three(0, 0, 8).start()
    arrived(gathered.at[0, 0, pl.ds(8, 8)], g1_recv.at[CHUNKS])
    gather_three(0, 8, 8).start()
    to_second(2)
    arrive(0)

    slots = lax.broadcasted_iota(jnp.int32, (1, SHARD), 1)

    def score(b, target):
        rows = []
        for s in range(S):
            r = b * S + s
            tiles = [
                query_f32[r // 16, t, pl.ds(r % 16, 32, stride=16), :] for t in range(WIDE // 128)
            ]
            rows.append(jnp.concatenate(tiles, axis=1)[:, :RANK])
        target[...] = dot(jnp.concatenate(rows, axis=0).astype(BF), cache[b], NN)

    def soften(b, source, target, stats):
        for s in range(S):
            last = lengths_ref[b] - S + s - kv * SHARD
            part = jnp.where(slots <= last, source[32 * s : 32 * s + 32, :], MASKED)
            top = jnp.max(part, axis=1, keepdims=True)
            weights = jnp.exp2((part - top) * FACTOR)
            total = jnp.sum(weights, axis=1, keepdims=True)
            target[32 * s : 32 * s + 32, :] = weights.astype(BF)
            stats[32 * s : 32 * s + 32, :] = stat_tile(top, total)

    def weigh(b, source, stats):
        numerators = dot(source[...], cache[b, :DC], NT)
        for s in range(S):
            r = b * S + s
            for t in range(DC // 128):
                partial[r // 16, t, pl.ds(r % 16, 32, stride=16), :] = numerators[
                    32 * s : 32 * s + 32, 128 * t : 128 * t + 128
                ]
            partial[r // 16, 4, pl.ds(r % 16, 32, stride=16), :] = stats[32 * s : 32 * s + 32, :]

    def pair_copy(k, start, count, channel):
        span = pl.ds(start, count)
        return remote(
            pair_send.at[k, span], pair_recv.at[k, span], pair_ss.at[k], pair_rs.at[channel], sibling
        )

    def first_copy(k, step):
        return remote(
            first_send.at[k, pl.ds(4 * step, 4)], first_recv.at[k, step - 1],
            r1_send.at[k], r1_recv.at[k], along_second(4 - step),
        )

    def second_copy(k, step):
        return remote(
            second_send.at[k, step], second_recv.at[k, step - 1],
            r2_send.at[k], r2_recv.at[k], along_first(4 - step),
        )

    def last_copy(peer):
        back = (4 - peer // 4) % 4 * 4 + (4 - peer % 4) % 4
        return remote(
            first_send.at[CHUNKS - 1, peer], last_recv.at[peer],
            r1_send.at[CHUNKS - 1], r1_recv.at[CHUNKS - 1], plane_peer(back),
        )

    def store_group(k, group, joined):
        tiles, top, total = joined
        tiles = tiles + [stat_tile(top, total)]
        for t in range(WIDE // 128):
            first_send[k, 4 * group : 4 * group + 4, :, 128 * t : 128 * t + 128] = (
                tiles[t].astype(BF).reshape(4, 16, 128)
            )

    def pack_pair(k, start, count):
        for t in range(WIDE // 128):
            pair_send[k, start : start + count, :, 128 * t : 128 * t + 128] = (
                partial[k, t, 256 + 16 * start : 256 + 16 * (start + count)]
                .astype(BF)
                .reshape(count, 16, 128)
            )

    def step_pair(k):
        pack_pair(k, 0, 16)
        pair_copy(k, 0, 16, k).start()

    def join_group(k, group):
        rows = slice(64 * group, 64 * group + 64)
        span = slice(4 * group, 4 * group + 4)
        own_part = (lambda t: partial[k, t, rows], partial[k, 4, rows])
        store_group(k, group, join([own_part, block_part(pair_recv, (k, span), 4)], spread))

    def step_first(k):
        arrived(pair_recv.at[k], pair_rs.at[k])
        for group in range(4):
            join_group(k, group)
        for step in (2, 1, 3):
            first_copy(k, step).start()

    def last_pair():
        for group in (2, 1, 3, 0):
            pack_pair(CHUNKS - 1, 4 * group, 4)
            pair_copy(CHUNKS - 1, 4 * group, 4, CHUNKS - 1 + group).start()

    def last_first():
        for group in (2, 1, 3, 0):
            arrived(pair_recv.at[CHUNKS - 1, pl.ds(4 * group, 4)], pair_rs.at[CHUNKS - 1 + group])
            join_group(CHUNKS - 1, group)
            for peer in range(max(1, 4 * group), 4 * group + 4):
                last_copy(peer).start()
        last_recv[0] = first_send[CHUNKS - 1, 0]

    def step_second(k):
        arrived(first_recv.at[k], r1_recv.at[k])
        parts = [block_part(first_send, (k, slice(0, 4)), 4)]
        parts += [block_part(first_recv, (k, step), 4) for step in range(3)]
        tiles, top, total = join(parts, spread)
        tiles = tiles + [stat_tile(top, total)]
        for t in range(WIDE // 128):
            second_send[k, :, :, 128 * t : 128 * t + 128] = tiles[t].astype(BF).reshape(4, 16, 128)
        for step in (2, 1, 3):
            second_copy(k, step).start()

    def step_last(k):
        if k < CHUNKS - 1:
            arrived(second_recv.at[k], r2_recv.at[k])
            parts = [block_part(second_send, (k, 0), 1)]
            parts += [block_part(second_recv, (k, step), 1) for step in range(3)]
            tiles, _, total = join(parts, spread)
        else:
            arrived(last_recv.at[pl.ds(1, 15)], r1_recv.at[k])
            tiles, _, total = join_stack(last_recv, spread)
        for t in range(DC // 128):
            latent[16 * k : 16 * k + 16, 128 * t : 128 * t + 128] = (tiles[t] / total).astype(BF)

    cache_copy(0).wait()
    score(0, scores_a)
    soften(0, scores_a, probs_a, stats_a)

    def after(b, schedule):
        for when, step, k in schedule:
            pl.when(b == when)(functools.partial(step, k))

    def rollout_pair(i, carry):
        b = 2 * i
        cache_copy(i + 1).wait()
        score(b + 1, scores_b)
        weigh(b, probs_a, stats_a)
        soften(b + 1, scores_b, probs_b, stats_b)
        after(b, [(6, to_sibling, 2), (8, arrive, 2), (8, step_first, 0), (10, step_pair, 1)])
        score(b + 2, scores_a)
        weigh(b + 1, probs_b, stats_b)
        soften(b + 2, scores_a, probs_a, stats_a)
        after(b + 1, [(1, to_sibling, 1), (3, arrive, 1), (5, step_pair, 0), (13, step_first, 1)])
        return carry

    lax.fori_loop(0, B // 2 - 1, rollout_pair, 0)
    score(B - 1, scores_b)
    weigh(B - 2, probs_a, stats_a)
    soften(B - 1, scores_b, probs_b, stats_b)
    weigh(B - 1, probs_b, stats_b)
    last_pair()
    step_second(0)
    last_first()
    step_second(1)
    step_last(0)
    step_last(1)
    step_last(2)

    small_copies[5].wait()

    head_values = dot(latent[...], value_ref[...], NN).astype(BF)
    back = jnp.where(line == (column % S) * B + column // S, 1.0, 0.0).astype(BF)
    values[0] = dot(back, head_values, NN).astype(BF)

    def values_copy(peer):
        return remote(
            values.at[0], values.at[peer], v_send.at[0], v_recv.at[0], column_peer(peer)
        )

    for peer in range(1, 8):
        values_copy(peer).start()
    arrived(weights_all.at[pl.ds(1, 7)], w_recv.at[0])
    arrived(values.at[pl.ds(1, 7)], v_recv.at[0])

    all_values = jnp.concatenate([values[peer] for peer in range(8)], axis=1)
    def out_copy(over, beside):
        return remote(
            out_send.at[over, lax.rem(z + beside, 4)], out_recv.at[4 * over + beside - 1],
            o_send.at[0], o_recv.at[0], place(x + over, z + beside, core, row_y),
        )

    for over in (2, 1, 3, 0):
        lanes = pl.ds(pl.multiple_of(256 * lax.rem(x + over, 4), 256), 256)
        features = dot(all_values, weights_all[:, :, lanes].reshape(8 * DN, 256), NN)
        for slot in range(4):
            piece = features[:, 64 * slot : 64 * slot + 64]
            out_send[over, slot] = jnp.concatenate(
                [
                    jnp.concatenate([piece[:16], piece[16:32]], axis=1),
                    jnp.concatenate([piece[32:], jnp.zeros((16, 64), F32)], axis=1),
                ],
                axis=0,
            ).astype(BF)
        for beside in (2, 1, 3, 0):
            if over or beside:
                out_copy(over, beside).start()
    total = out_send[0, z].astype(F32)
    arrived(out_recv, o_recv.at[0])
    for peer in range(1, 16):
        total = total + out_recv[peer - 1].astype(F32)
    out_ref[...] = jnp.concatenate(
        [total[:16, :FEAT], total[:16, 64 : 64 + FEAT], total[16:, :FEAT]], axis=0
    ).astype(BF)

    for k in range(CHUNKS):
        departed(gathered.at[0, k, pl.ds(1, 15 if k == 0 else 3)], g1_send.at[k])
        departed(gathered.at[0, k], g3_send.at[k])
        departed(pair_recv.at[k], pair_ss.at[k])
        if k > 0:
            departed(gathered.at[0, k, pl.ds(4, 12)], g2_send.at[k])
        if k < CHUNKS - 1:
            departed(first_recv.at[k], r1_send.at[k])
            departed(second_recv.at[k], r2_send.at[k])
        else:
            departed(last_recv.at[pl.ds(1, 15)], r1_send.at[k])
    departed(weights_all.at[pl.ds(1, 7)], w_send.at[0])
    departed(values.at[pl.ds(1, 7)], v_send.at[0])
    departed(out_recv, o_send.at[0])


def body(query_heads, key_up, value_up, output_weight, latent_cache, lengths, positions):
    query = jnp.transpose(query_heads[:, :, 0, :], (1, 0, 2)).reshape(ROWS, DN + DR)
    cache = jnp.swapaxes(latent_cache, 1, 2)
    width = output_weight.shape[1]
    dma = pltpu.SemaphoreType.DMA
    vmem, smem = pltpu.VMEM, pltpu.SMEM
    out = pl.pallas_call(
        kernel,
        out_shape=jax.ShapeDtypeStruct((ROWS, FEAT), BF),
        in_specs=[
            pl.BlockSpec(memory_space=pl.ANY) for _ in range(7)
        ],
        out_specs=pl.BlockSpec(memory_space=vmem),
        scratch_shapes=[
            smem((B,), jnp.int32),
            smem((B,), jnp.int32),
            vmem((ROWS, DN + DR), BF),
            vmem((DN, DC), BF),
            vmem((DC, 128), BF),
            vmem((B, RANK, SHARD), BF),
            vmem((DN, width), BF),
            vmem((2, 4, DN, 1024), BF),
            vmem((8, DN, 1024), BF),
            vmem((2, CHUNKS, 16, 16, WIDE), BF),
            vmem((CHUNKS, WIDE // 128, 512, 128), F32),
            vmem((96, SHARD), F32),
            vmem((96, SHARD), F32),
            vmem((96, SHARD), BF),
            vmem((96, SHARD), BF),
            vmem((96, 128), F32),
            vmem((96, 128), F32),
            vmem((CHUNKS, WIDE // 128, 512, 128), F32),
            vmem((CHUNKS, 16, 16, WIDE), BF),
            vmem((CHUNKS, 16, 16, WIDE), BF),
            vmem((CHUNKS, 16, 16, WIDE), BF),
            vmem((CHUNKS, 3, 4, 16, WIDE), BF),
            vmem((CHUNKS, 4, 16, WIDE), BF),
            vmem((CHUNKS, 3, 16, WIDE), BF),
            vmem((ROWS, DC), BF),
            vmem((8, ROWS, 128), BF),
            vmem((4, 4, 32, 128), BF),
            vmem((15, 32, 128), BF),
            vmem((16, 16, WIDE), BF),
            vmem((128, 256), BF),
            dma((B // 2,)),
            dma((6,)),
            dma((CHUNKS,)), dma((CHUNKS + 1,)),
            dma((CHUNKS,)), dma((CHUNKS,)),
            dma((CHUNKS,)), dma((CHUNKS,)),
            dma((CHUNKS,)), dma((CHUNKS + 3,)),
            dma((CHUNKS,)), dma((CHUNKS,)),
            dma((CHUNKS,)), dma((CHUNKS,)),
            dma((1,)), dma((1,)),
            dma((1,)), dma((1,)),
            dma((1,)), dma((1,)),
        ],
        compiler_params=pltpu.CompilerParams(
            collective_id=0, has_side_effects=True, vmem_limit_bytes=56 * 2**20
        ),
    )(lengths, positions, query, key_up[0], value_up[0], output_weight, cache)
    return jnp.transpose(out.reshape(S, B, FEAT), (1, 0, 2))


def solution(mesh):
    in_specs = (
        P(None, None, ("kv", "head"), None),
        P(("kv", "head"), None, None),
        P(("kv", "head"), None, None),
        P(("kv", "head"), None),
        P(None, "kv", None),
        P(),
        P(),
    )
    out_specs = P(None, None, ("kv", "head"))
    return jax.shard_map(body, mesh=mesh, in_specs=in_specs, out_specs=out_specs, check_vma=False)
```

```python
import functools

import jax
import jax.numpy as jnp
import numpy as np
from jax import lax
from jax.experimental import pallas as pl
from jax.experimental.pallas import tpu as pltpu
from jax.sharding import PartitionSpec as P

MESH = pl.DeviceIdType.MESH
BF = jnp.bfloat16
F32 = jnp.float32

DN = 128
DR = 64
DC = 512
B = 16
S = 3
ROWS = B * S
CHUNKS = ROWS // 16
RANK = DC + DR
WIDE = 640
SHARD = 1024
FEAT = 56
MASKED = -(2.0**100)
PLANE_ORDER = (10, 6, 9, 11, 14, 2, 8, 5, 7, 13, 15, 1, 3, 4, 12)
FACTOR = float(np.log2(np.e) / np.sqrt(DN + DR))

dot = functools.partial(lax.dot_general, preferred_element_type=F32)
NN = (((1,), (0,)), ((), ()))
NT = (((1,), (1,)), ((), ()))


def split3(value):
    high = value.astype(BF).astype(F32)
    rest = value - high
    middle = rest.astype(BF).astype(F32)
    return high, middle, rest - middle


def stat_tile(top, total):
    lane = lax.broadcasted_iota(jnp.int32, (top.shape[0], 128), 1)
    top_high, top_middle, top_low = split3(top)
    total_high, total_middle, _ = split3(total)
    tile = jnp.where(lane == 4, total_middle, 0.0)
    tile = jnp.where(lane == 3, total_high, tile)
    tile = jnp.where(lane == 2, top_low, tile)
    tile = jnp.where(lane == 1, top_middle, tile)
    return jnp.where(lane == 0, top_high, tile)


def spread_matrix():
    source = lax.broadcasted_iota(jnp.int32, (128, 256), 0)
    target = lax.broadcasted_iota(jnp.int32, (128, 256), 1)
    is_top = (source < 3) & (target < 128)
    is_total = (source >= 3) & (source < 5) & (target >= 128)
    return jnp.where(is_top | is_total, 1.0, 0.0).astype(BF)


def spread_stats(tile, spread):
    both = dot(tile.astype(BF), spread[...], NN)
    return both[:, :128], both[:, 128:]


def join(parts, spread):
    stats = [spread_stats(tile, spread) for _, tile in parts]
    top = functools.reduce(jnp.maximum, [m for m, _ in stats])
    factors = [jnp.exp2((m - top) * FACTOR) for m, _ in stats]
    total = sum(f * l for f, (_, l) in zip(factors, stats))
    tiles = []
    for t in range(DC // 128):
        tiles.append(sum(f * data(t) for f, (data, _) in zip(factors, parts)))
    return tiles, top, total


def join_stack(ref, spread):
    count = ref.shape[0]
    tops, totals = spread_stats(ref[:, :, DC:].reshape(count * 16, 128), spread)
    tops = tops.reshape(count, 16, 128)
    top = jnp.max(tops, axis=0)
    factors = jnp.exp2((tops - top[None]) * FACTOR)
    total = jnp.sum(factors * totals.reshape(count, 16, 128), axis=0)
    tiles = [
        jnp.sum(factors * ref[:, :, 128 * t : 128 * t + 128].astype(F32), axis=0)
        for t in range(DC // 128)
    ]
    return tiles, top, total


def block_part(ref, index, count):
    rows = count * 16

    def data(t):
        return ref[index][..., 128 * t : 128 * t + 128].astype(F32).reshape(rows, 128)

    return data, ref[index][..., DC:WIDE].reshape(rows, 128)


def kernel(
    lengths_hbm, positions_hbm, query_hbm, key_hbm, value_hbm, weight_hbm, cache_hbm, out_ref,
    lengths_ref, positions_ref, query_ref, key_ref, value_ref,
    cache, weight, wide, weights_all, gathered, query_f32, scores_a, scores_b, probs_a, probs_b,
    stats_a, stats_b, partial, pair_send, pair_recv, first_send, first_recv, second_send, second_recv,
    latent, values, out_send, out_recv,
    last_recv, spread, cache_sem, small_sem, g1_send, g1_recv, g2_send, g2_recv, g3_send, g3_recv,
    pair_ss, pair_rs, r1_send, r1_recv, r2_send, r2_recv, w_send, w_recv, v_send, v_recv, o_send, o_recv,
):
    kv = lax.axis_index("kv")
    row_y = lax.axis_index("head")
    x, z, core = kv // 8, (kv // 2) % 4, kv % 2

    def place(px, pz, pc, py):
        return (lax.rem(px, 4) * 8 + lax.rem(pz, 4) * 2 + pc, lax.rem(py, 4))

    def along_first(step):
        return plane_peer(step)

    def along_second(step):
        return plane_peer(4 * step)

    def column_peer(peer):
        return place(x, z, lax.rem(core + peer // 4, 2), row_y + peer % 4)

    def plane_peer(peer):
        first, second = peer % 4, peer // 4
        return place(
            x + first * (1 - core) + second * core, z + second * (1 - core) + first * core, core, row_y
        )

    sibling = place(x, z, 1 - core, row_y)

    def remote(src, dst, send, recv, device):
        return pltpu.make_async_remote_copy(
            src_ref=src, dst_ref=dst, send_sem=send, recv_sem=recv,
            device_id=device, device_id_type=MESH,
        )

    def arrived(ref, semaphore):
        remote(ref, ref, semaphore, semaphore, sibling).wait_recv()

    def departed(ref, semaphore):
        remote(ref, ref, semaphore, semaphore, sibling).wait_send()

    def cache_copy(pair):
        span = pl.ds(2 * pair, 2)
        return pltpu.make_async_copy(cache_hbm.at[span], cache.at[span], cache_sem.at[pair])

    small_copies = [
        pltpu.make_async_copy(source, target, small_sem.at[i])
        for i, (source, target) in enumerate([
            (positions_hbm, positions_ref), (query_hbm, query_ref), (key_hbm, key_ref),
            (lengths_hbm, lengths_ref), (weight_hbm, weight), (value_hbm, value_ref),
        ])
    ]

    barrier = pltpu.get_barrier_semaphore()
    partners = [plane_peer(peer) for peer in PLANE_ORDER] + [column_peer(peer) for peer in range(1, 8)]
    for partner in partners:
        pl.semaphore_signal(barrier, inc=1, device_id=partner, device_id_type=MESH)
    for copy in small_copies:
        copy.start()
    for pair in range(B // 2):
        cache_copy(pair).start()

    spread[...] = spread_matrix()

    for copy in small_copies[:4]:
        copy.wait()
    line = lax.broadcasted_iota(jnp.int32, (ROWS, ROWS), 0)
    column = lax.broadcasted_iota(jnp.int32, (ROWS, ROWS), 1)
    reorder = jnp.where(column == (line % S) * B + line // S, 1.0, 0.0).astype(BF)
    query = dot(reorder, query_ref[...], NN)
    query_latent = dot(query[:, :DN].astype(BF), key_ref[...], NN)
    lane = lax.broadcasted_iota(jnp.int32, (ROWS, DR // 2), 1).astype(F32)
    frequency = jnp.exp(lane * (-np.log(10000.0) / (DR // 2)))
    token_row = lax.broadcasted_iota(jnp.int32, (ROWS, DR // 2), 0)
    spot = jnp.zeros((ROWS, DR // 2), jnp.int32)
    for b in range(B):
        spot = jnp.where(token_row // S == b, positions_ref[b], spot)
    angle = (spot + token_row % S).astype(F32) * frequency
    cosine, sine = jnp.cos(angle), jnp.sin(angle)
    first_half, second_half = query[:, DN : DN + DR // 2], query[:, DN + DR // 2 :]
    own = jnp.concatenate(
        [
            query_latent,
            first_half * cosine - second_half * sine,
            second_half * cosine + first_half * sine,
            jnp.zeros((ROWS, WIDE - RANK), F32),
        ],
        axis=1,
    ).astype(BF)
    for k in range(CHUNKS):
        gathered[0, k, 0] = own[16 * k : 16 * k + 16]

    pl.semaphore_wait(barrier, len(partners))

    def gather_one(k, peer):
        return remote(
            gathered.at[0, k, 0], gathered.at[0, k, peer], g1_send.at[k],
            g1_recv.at[CHUNKS if k == 0 and peer >= 8 else k], plane_peer(peer),
        )

    def gather_two(k, step):
        return remote(
            gathered.at[0, k, pl.ds(0, 4)], gathered.at[0, k, pl.ds(4 * step, 4)],
            g2_send.at[k], g2_recv.at[k], along_second(step),
        )

    def gather_three(k, start, count):
        span = pl.ds(start, count)
        return remote(
            gathered.at[0, k, span], gathered.at[1, k, span], g3_send.at[k], g3_recv.at[k], sibling
        )

    for step in (2, 1, 3):
        gather_one(1, step).start()
    for peer in (2, 5, 6, 7, 1, 3, 4, 10, 8, 9, 11, 14, 13, 15, 12):
        gather_one(0, peer).start()
    for step in (2, 1, 3):
        gather_one(2, step).start()

    small_copies[4].wait()

    def widen(g, carry):
        base = pl.multiple_of(g * (16 * FEAT), 128)
        strip = weight[:, pl.ds(base, 16 * FEAT)]
        gap = jnp.zeros((DN, 64 - FEAT), BF)
        for parity in range(2):
            for side in range(4):
                start = (parity * 4 + side) * FEAT
                wide[parity, side, :, pl.ds(pl.multiple_of(g * 128, 128), 128)] = jnp.concatenate(
                    [strip[:, start : start + FEAT], gap,
                     strip[:, start + 8 * FEAT : start + 9 * FEAT], gap], axis=1)
        return carry

    lax.fori_loop(0, 8, widen, 0)

    def weight_send(peer):
        turn, step = peer // 4, peer % 4
        return remote(
            wide.at[lax.rem(core + turn, 2), lax.rem(row_y + step, 4)], weights_all.at[peer],
            w_send.at[0], w_recv.at[0], column_peer(peer),
        )

    for peer in range(1, 8):
        weight_send(peer).start()
    weights_all[0] = wide[core, row_y]

    def to_second(k):
        arrived(gathered.at[0, k, pl.ds(1, 3)], g1_recv.at[k])
        for step in (2, 1, 3):
            gather_two(k, step).start()
        gather_three(k, 0, 4).start()

    def to_sibling(k):
        arrived(gathered.at[0, k, pl.ds(4, 12)], g2_recv.at[k])
        gather_three(k, 4, 12).start()

    def unpack(k, parity):
        for t in range(WIDE // 128):
            query_f32[k, t, parity * 256 : parity * 256 + 256] = (
                gathered[parity, k, :, :, 128 * t : 128 * t + 128].astype(F32).reshape(256, 128)
            )

    def arrive(k):
        unpack(k, 0)
        arrived(gathered.at[1, k], g3_recv.at[k])
        unpack(k, 1)

    to_second(1)
    arrived(gathered.at[0, 0, pl.ds(1, 7)], g1_recv.at[0])
    gather_three(0, 0, 8).start()
    arrived(gathered.at[0, 0, pl.ds(8, 8)], g1_recv.at[CHUNKS])
    gather_three(0, 8, 8).start()
    to_second(2)
    arrive(0)

    slots = lax.broadcasted_iota(jnp.int32, (1, SHARD), 1)

    def score(b, target):
        rows = []
        for s in range(S):
            r = b * S + s
            tiles = [
                query_f32[r // 16, t, pl.ds(r % 16, 32, stride=16), :] for t in range(WIDE // 128)
            ]
            rows.append(jnp.concatenate(tiles, axis=1)[:, :RANK])
        target[...] = dot(jnp.concatenate(rows, axis=0).astype(BF), cache[b], NN)

    def soften(b, source, target, stats):
        for s in range(S):
            last = lengths_ref[b] - S + s - kv * SHARD
            part = jnp.where(slots <= last, source[32 * s : 32 * s + 32, :], MASKED)
            top = jnp.max(part, axis=1, keepdims=True)
            weights = jnp.exp2((part - top) * FACTOR)
            total = jnp.sum(weights, axis=1, keepdims=True)
            target[32 * s : 32 * s + 32, :] = weights.astype(BF)
            stats[32 * s : 32 * s + 32, :] = stat_tile(top, total)

    def weigh(b, source, stats):
        numerators = dot(source[...], cache[b, :DC], NT)
        for s in range(S):
            r = b * S + s
            for t in range(DC // 128):
                partial[r // 16, t, pl.ds(r % 16, 32, stride=16), :] = numerators[
                    32 * s : 32 * s + 32, 128 * t : 128 * t + 128
                ]
            partial[r // 16, 4, pl.ds(r % 16, 32, stride=16), :] = stats[32 * s : 32 * s + 32, :]

    def pair_copy(k, start, count, channel):
        span = pl.ds(start, count)
        return remote(
            pair_send.at[k, span], pair_recv.at[k, span], pair_ss.at[k], pair_rs.at[channel], sibling
        )

    def first_copy(k, step):
        return remote(
            first_send.at[k, pl.ds(4 * step, 4)], first_recv.at[k, step - 1],
            r1_send.at[k], r1_recv.at[k], along_second(4 - step),
        )

    def second_copy(k, step):
        return remote(
            second_send.at[k, step], second_recv.at[k, step - 1],
            r2_send.at[k], r2_recv.at[k], along_first(4 - step),
        )

    def last_copy(peer):
        back = (4 - peer // 4) % 4 * 4 + (4 - peer % 4) % 4
        return remote(
            first_send.at[CHUNKS - 1, peer], last_recv.at[peer],
            r1_send.at[CHUNKS - 1], r1_recv.at[CHUNKS - 1], plane_peer(back),
        )

    def store_group(k, group, joined):
        tiles, top, total = joined
        tiles = tiles + [stat_tile(top, total)]
        for t in range(WIDE // 128):
            first_send[k, 4 * group : 4 * group + 4, :, 128 * t : 128 * t + 128] = (
                tiles[t].astype(BF).reshape(4, 16, 128)
            )

    def pack_pair(k, start, count):
        for t in range(WIDE // 128):
            pair_send[k, start : start + count, :, 128 * t : 128 * t + 128] = (
                partial[k, t, 256 + 16 * start : 256 + 16 * (start + count)]
                .astype(BF)
                .reshape(count, 16, 128)
            )

    def step_pair(k):
        pack_pair(k, 0, 16)
        pair_copy(k, 0, 16, k).start()

    def join_group(k, group):
        rows = slice(64 * group, 64 * group + 64)
        span = slice(4 * group, 4 * group + 4)
        own_part = (lambda t: partial[k, t, rows], partial[k, 4, rows])
        store_group(k, group, join([own_part, block_part(pair_recv, (k, span), 4)], spread))

    def step_first(k):
        arrived(pair_recv.at[k], pair_rs.at[k])
        for group in range(4):
            join_group(k, group)
        for step in (2, 1, 3):
            first_copy(k, step).start()

    def last_pair():
        for group in (2, 1, 3, 0):
            pack_pair(CHUNKS - 1, 4 * group, 4)
            pair_copy(CHUNKS - 1, 4 * group, 4, CHUNKS - 1 + group).start()

    def last_first():
        for group in (2, 1, 3, 0):
            arrived(pair_recv.at[CHUNKS - 1, pl.ds(4 * group, 4)], pair_rs.at[CHUNKS - 1 + group])
            join_group(CHUNKS - 1, group)
            for peer in range(max(1, 4 * group), 4 * group + 4):
                last_copy(peer).start()
        last_recv[0] = first_send[CHUNKS - 1, 0]

    def step_second(k):
        arrived(first_recv.at[k], r1_recv.at[k])
        parts = [block_part(first_send, (k, slice(0, 4)), 4)]
        parts += [block_part(first_recv, (k, step), 4) for step in range(3)]
        tiles, top, total = join(parts, spread)
        tiles = tiles + [stat_tile(top, total)]
        for t in range(WIDE // 128):
            second_send[k, :, :, 128 * t : 128 * t + 128] = tiles[t].astype(BF).reshape(4, 16, 128)
        for step in (2, 1, 3):
            second_copy(k, step).start()

    def step_last(k):
        if k < CHUNKS - 1:
            arrived(second_recv.at[k], r2_recv.at[k])
            parts = [block_part(second_send, (k, 0), 1)]
            parts += [block_part(second_recv, (k, step), 1) for step in range(3)]
            tiles, _, total = join(parts, spread)
        else:
            arrived(last_recv.at[pl.ds(1, 15)], r1_recv.at[k])
            tiles, _, total = join_stack(last_recv, spread)
        for t in range(DC // 128):
            latent[16 * k : 16 * k + 16, 128 * t : 128 * t + 128] = (tiles[t] / total).astype(BF)

    cache_copy(0).wait()
    score(0, scores_a)
    soften(0, scores_a, probs_a, stats_a)

    def after(b, schedule):
        for when, step, k in schedule:
            if b == when:
                step(k)

    def rollout_pair(i, carry):
        b = 2 * i
        cache_copy(i + 1).wait()
        score(b + 1, scores_b)
        weigh(b, probs_a, stats_a)
        soften(b + 1, scores_b, probs_b, stats_b)
        after(b, [(6, to_sibling, 2), (8, arrive, 2), (8, step_first, 0), (10, step_pair, 1)])
        score(b + 2, scores_a)
        weigh(b + 1, probs_b, stats_b)
        soften(b + 2, scores_a, probs_a, stats_a)
        after(b + 1, [(1, to_sibling, 1), (3, arrive, 1), (5, step_pair, 0), (13, step_first, 1)])
        return carry

    for i in range(B // 2 - 1):
        rollout_pair(i, 0)
    score(B - 1, scores_b)
    weigh(B - 2, probs_a, stats_a)
    soften(B - 1, scores_b, probs_b, stats_b)
    weigh(B - 1, probs_b, stats_b)
    last_pair()
    step_second(0)
    last_first()
    step_second(1)
    step_last(0)
    step_last(1)
    step_last(2)

    small_copies[5].wait()

    head_values = dot(latent[...], value_ref[...], NN).astype(BF)
    back = jnp.where(line == (column % S) * B + column // S, 1.0, 0.0).astype(BF)
    values[0] = dot(back, head_values, NN).astype(BF)

    def values_copy(peer):
        return remote(
            values.at[0], values.at[peer], v_send.at[0], v_recv.at[0], column_peer(peer)
        )

    for peer in range(1, 8):
        values_copy(peer).start()
    arrived(weights_all.at[pl.ds(1, 7)], w_recv.at[0])
    arrived(values.at[pl.ds(1, 7)], v_recv.at[0])

    all_values = jnp.concatenate([values[peer] for peer in range(8)], axis=1)
    def out_copy(over, beside):
        return remote(
            out_send.at[over, lax.rem(z + beside, 4)], out_recv.at[4 * over + beside - 1],
            o_send.at[0], o_recv.at[0], place(x + over, z + beside, core, row_y),
        )

    for over in (2, 1, 3, 0):
        lanes = pl.ds(pl.multiple_of(256 * lax.rem(x + over, 4), 256), 256)
        features = dot(all_values, weights_all[:, :, lanes].reshape(8 * DN, 256), NN)
        for slot in range(4):
            piece = features[:, 64 * slot : 64 * slot + 64]
            out_send[over, slot] = jnp.concatenate(
                [
                    jnp.concatenate([piece[:16], piece[16:32]], axis=1),
                    jnp.concatenate([piece[32:], jnp.zeros((16, 64), F32)], axis=1),
                ],
                axis=0,
            ).astype(BF)
        for beside in (2, 1, 3, 0):
            if over or beside:
                out_copy(over, beside).start()
    total = out_send[0, z].astype(F32)
    arrived(out_recv, o_recv.at[0])
    for peer in range(1, 16):
        total = total + out_recv[peer - 1].astype(F32)
    out_ref[...] = jnp.concatenate(
        [total[:16, :FEAT], total[:16, 64 : 64 + FEAT], total[16:, :FEAT]], axis=0
    ).astype(BF)

    for k in range(CHUNKS):
        departed(gathered.at[0, k, pl.ds(1, 15 if k == 0 else 3)], g1_send.at[k])
        departed(gathered.at[0, k], g3_send.at[k])
        departed(pair_recv.at[k], pair_ss.at[k])
        if k > 0:
            departed(gathered.at[0, k, pl.ds(4, 12)], g2_send.at[k])
        if k < CHUNKS - 1:
            departed(first_recv.at[k], r1_send.at[k])
            departed(second_recv.at[k], r2_send.at[k])
        else:
            departed(last_recv.at[pl.ds(1, 15)], r1_send.at[k])
    departed(weights_all.at[pl.ds(1, 7)], w_send.at[0])
    departed(values.at[pl.ds(1, 7)], v_send.at[0])
    departed(out_recv, o_send.at[0])


def body(query_heads, key_up, value_up, output_weight, latent_cache, lengths, positions):
    query = jnp.transpose(query_heads[:, :, 0, :], (1, 0, 2)).reshape(ROWS, DN + DR)
    cache = jnp.swapaxes(latent_cache, 1, 2)
    width = output_weight.shape[1]
    dma = pltpu.SemaphoreType.DMA
    vmem, smem = pltpu.VMEM, pltpu.SMEM
    out = pl.pallas_call(
        kernel,
        out_shape=jax.ShapeDtypeStruct((ROWS, FEAT), BF),
        in_specs=[
            pl.BlockSpec(memory_space=pl.ANY) for _ in range(7)
        ],
        out_specs=pl.BlockSpec(memory_space=vmem),
        scratch_shapes=[
            smem((B,), jnp.int32),
            smem((B,), jnp.int32),
            vmem((ROWS, DN + DR), BF),
            vmem((DN, DC), BF),
            vmem((DC, 128), BF),
            vmem((B, RANK, SHARD), BF),
            vmem((DN, width), BF),
            vmem((2, 4, DN, 1024), BF),
            vmem((8, DN, 1024), BF),
            vmem((2, CHUNKS, 16, 16, WIDE), BF),
            vmem((CHUNKS, WIDE // 128, 512, 128), F32),
            vmem((96, SHARD), F32),
            vmem((96, SHARD), F32),
            vmem((96, SHARD), BF),
            vmem((96, SHARD), BF),
            vmem((96, 128), F32),
            vmem((96, 128), F32),
            vmem((CHUNKS, WIDE // 128, 512, 128), F32),
            vmem((CHUNKS, 16, 16, WIDE), BF),
            vmem((CHUNKS, 16, 16, WIDE), BF),
            vmem((CHUNKS, 16, 16, WIDE), BF),
            vmem((CHUNKS, 3, 4, 16, WIDE), BF),
            vmem((CHUNKS, 4, 16, WIDE), BF),
            vmem((CHUNKS, 3, 16, WIDE), BF),
            vmem((ROWS, DC), BF),
            vmem((8, ROWS, 128), BF),
            vmem((4, 4, 32, 128), BF),
            vmem((15, 32, 128), BF),
            vmem((16, 16, WIDE), BF),
            vmem((128, 256), BF),
            dma((B // 2,)),
            dma((6,)),
            dma((CHUNKS,)), dma((CHUNKS + 1,)),
            dma((CHUNKS,)), dma((CHUNKS,)),
            dma((CHUNKS,)), dma((CHUNKS,)),
            dma((CHUNKS,)), dma((CHUNKS + 3,)),
            dma((CHUNKS,)), dma((CHUNKS,)),
            dma((CHUNKS,)), dma((CHUNKS,)),
            dma((1,)), dma((1,)),
            dma((1,)), dma((1,)),
            dma((1,)), dma((1,)),
        ],
        compiler_params=pltpu.CompilerParams(
            collective_id=0, has_side_effects=True, vmem_limit_bytes=56 * 2**20
        ),
    )(lengths, positions, query, key_up[0], value_up[0], output_weight, cache)
    return jnp.transpose(out.reshape(S, B, FEAT), (1, 0, 2))


def solution(mesh):
    in_specs = (
        P(None, None, ("kv", "head"), None),
        P(("kv", "head"), None, None),
        P(("kv", "head"), None, None),
        P(("kv", "head"), None),
        P(None, "kv", None),
        P(),
        P(),
    )
    out_specs = P(None, None, ("kv", "head"))
    return jax.shard_map(body, mesh=mesh, in_specs=in_specs, out_specs=out_specs, check_vma=False)
```

```python
import functools

import jax
import jax.numpy as jnp
import numpy as np
from jax import lax
from jax.experimental import pallas as pl
from jax.experimental.pallas import tpu as pltpu
from jax.sharding import PartitionSpec as P

MESH = pl.DeviceIdType.MESH
BF = jnp.bfloat16
F32 = jnp.float32

DN = 128
DR = 64
DC = 512
B = 16
S = 3
ROWS = B * S
CHUNKS = ROWS // 16
RANK = DC + DR
WIDE = 640
SHARD = 1024
FEAT = 56
MASKED = -(2.0**100)
PLANE_ORDER = (10, 6, 9, 11, 14, 2, 8, 5, 7, 13, 15, 1, 3, 4, 12)
FACTOR = float(np.log2(np.e) / np.sqrt(DN + DR))

dot = functools.partial(lax.dot_general, preferred_element_type=F32)
NN = (((1,), (0,)), ((), ()))
NT = (((1,), (1,)), ((), ()))


def split3(value):
    high = value.astype(BF).astype(F32)
    rest = value - high
    middle = rest.astype(BF).astype(F32)
    return high, middle, rest - middle


def stat_tile(top, total):
    lane = lax.broadcasted_iota(jnp.int32, (top.shape[0], 128), 1)
    top_high, top_middle, top_low = split3(top)
    total_high, total_middle, _ = split3(total)
    tile = jnp.where(lane == 4, total_middle, 0.0)
    tile = jnp.where(lane == 3, total_high, tile)
    tile = jnp.where(lane == 2, top_low, tile)
    tile = jnp.where(lane == 1, top_middle, tile)
    return jnp.where(lane == 0, top_high, tile)


def spread_matrix():
    source = lax.broadcasted_iota(jnp.int32, (128, 256), 0)
    target = lax.broadcasted_iota(jnp.int32, (128, 256), 1)
    is_top = (source < 3) & (target < 128)
    is_total = (source >= 3) & (source < 5) & (target >= 128)
    return jnp.where(is_top | is_total, 1.0, 0.0).astype(BF)


def spread_stats(tile, spread):
    both = dot(tile.astype(BF), spread[...], NN)
    return both[:, :128], both[:, 128:]


def join(parts, spread):
    stats = [spread_stats(tile, spread) for _, tile in parts]
    top = functools.reduce(jnp.maximum, [m for m, _ in stats])
    factors = [jnp.exp2((m - top) * FACTOR) for m, _ in stats]
    total = sum(f * l for f, (_, l) in zip(factors, stats))
    tiles = []
    for t in range(DC // 128):
        tiles.append(sum(f * data(t) for f, (data, _) in zip(factors, parts)))
    return tiles, top, total


def join_stack(ref, spread):
    count = ref.shape[0]
    tops, totals = spread_stats(ref[:, :, DC:].reshape(count * 16, 128), spread)
    tops = tops.reshape(count, 16, 128)
    top = jnp.max(tops, axis=0)
    factors = jnp.exp2((tops - top[None]) * FACTOR)
    total = jnp.sum(factors * totals.reshape(count, 16, 128), axis=0)
    tiles = [
        jnp.sum(factors * ref[:, :, 128 * t : 128 * t + 128].astype(F32), axis=0)
        for t in range(DC // 128)
    ]
    return tiles, top, total


def block_part(ref, index, count):
    rows = count * 16

    def data(t):
        return ref[index][..., 128 * t : 128 * t + 128].astype(F32).reshape(rows, 128)

    return data, ref[index][..., DC:WIDE].reshape(rows, 128)


def kernel(
    lengths_hbm, positions_hbm, query_hbm, key_hbm, value_hbm, weight_hbm, cache_hbm, out_ref,
    lengths_ref, positions_ref, query_ref, key_ref, value_ref,
    cache, weight, wide, weights_all, gathered, query_f32, scores_a, scores_b, probs_a, probs_b,
    stats_a, stats_b, partial, pair_send, pair_recv, first_send, first_recv, second_send, second_recv,
    latent, values, out_send, out_recv,
    last_recv, spread, cache_sem, small_sem, g1_send, g1_recv, g2_send, g2_recv, g3_send, g3_recv,
    pair_ss, pair_rs, r1_send, r1_recv, r2_send, r2_recv, w_send, w_recv, v_send, v_recv, o_send, o_recv,
):
    kv = lax.axis_index("kv")
    row_y = lax.axis_index("head")
    x, z, core = kv // 8, (kv // 2) % 4, kv % 2

    def place(px, pz, pc, py):
        return (lax.rem(px, 4) * 8 + lax.rem(pz, 4) * 2 + pc, lax.rem(py, 4))

    def along_first(step):
        return plane_peer(step)

    def along_second(step):
        return plane_peer(4 * step)

    def column_peer(peer):
        return place(x, z, lax.rem(core + peer // 4, 2), row_y + peer % 4)

    def plane_peer(peer):
        first, second = peer % 4, peer // 4
        return place(
            x + first * (1 - core) + second * core, z + second * (1 - core) + first * core, core, row_y
        )

    sibling = place(x, z, 1 - core, row_y)

    def remote(src, dst, send, recv, device):
        return pltpu.make_async_remote_copy(
            src_ref=src, dst_ref=dst, send_sem=send, recv_sem=recv,
            device_id=device, device_id_type=MESH,
        )

    def arrived(ref, semaphore):
        remote(ref, ref, semaphore, semaphore, sibling).wait_recv()

    def departed(ref, semaphore):
        remote(ref, ref, semaphore, semaphore, sibling).wait_send()

    def cache_copy(pair):
        span = pl.ds(2 * pair, 2)
        return pltpu.make_async_copy(cache_hbm.at[span], cache.at[span], cache_sem.at[pair])

    small_copies = [
        pltpu.make_async_copy(source, target, small_sem.at[i])
        for i, (source, target) in enumerate([
            (positions_hbm, positions_ref), (query_hbm, query_ref), (key_hbm, key_ref),
            (lengths_hbm, lengths_ref), (weight_hbm, weight), (value_hbm, value_ref),
        ])
    ]

    barrier = pltpu.get_barrier_semaphore()
    partners = [plane_peer(peer) for peer in PLANE_ORDER] + [column_peer(peer) for peer in range(1, 8)]
    for partner in partners:
        pl.semaphore_signal(barrier, inc=1, device_id=partner, device_id_type=MESH)
    for copy in small_copies:
        copy.start()
    for pair in range(B // 2):
        cache_copy(pair).start()

    spread[...] = spread_matrix()

    for copy in small_copies[:4]:
        copy.wait()
    line = lax.broadcasted_iota(jnp.int32, (ROWS, ROWS), 0)
    column = lax.broadcasted_iota(jnp.int32, (ROWS, ROWS), 1)
    reorder = jnp.where(column == (line % S) * B + line // S, 1.0, 0.0).astype(BF)
    query = dot(reorder, query_ref[...], NN)
    query_latent = dot(query[:, :DN].astype(BF), key_ref[...], NN)
    lane = lax.broadcasted_iota(jnp.int32, (ROWS, DR // 2), 1).astype(F32)
    frequency = jnp.exp(lane * (-np.log(10000.0) / (DR // 2)))
    token_row = lax.broadcasted_iota(jnp.int32, (ROWS, DR // 2), 0)
    spot = jnp.zeros((ROWS, DR // 2), jnp.int32)
    for b in range(B):
        spot = jnp.where(token_row // S == b, positions_ref[b], spot)
    angle = (spot + token_row % S).astype(F32) * frequency
    cosine, sine = jnp.cos(angle), jnp.sin(angle)
    first_half, second_half = query[:, DN : DN + DR // 2], query[:, DN + DR // 2 :]
    own = jnp.concatenate(
        [
            query_latent,
            first_half * cosine - second_half * sine,
            second_half * cosine + first_half * sine,
            jnp.zeros((ROWS, WIDE - RANK), F32),
        ],
        axis=1,
    ).astype(BF)
    for k in range(CHUNKS):
        gathered[0, k, 0] = own[16 * k : 16 * k + 16]

    pl.semaphore_wait(barrier, len(partners))

    def gather_one(k, peer):
        return remote(
            gathered.at[0, k, 0], gathered.at[0, k, peer], g1_send.at[k],
            g1_recv.at[CHUNKS if k == 0 and peer >= 8 else k], plane_peer(peer),
        )

    def gather_two(k, step):
        return remote(
            gathered.at[0, k, pl.ds(0, 4)], gathered.at[0, k, pl.ds(4 * step, 4)],
            g2_send.at[k], g2_recv.at[k], along_second(step),
        )

    def gather_three(k, start, count):
        span = pl.ds(start, count)
        return remote(
            gathered.at[0, k, span], gathered.at[1, k, span], g3_send.at[k], g3_recv.at[k], sibling
        )

    for step in (2, 1, 3):
        gather_one(1, step).start()
    for peer in (2, 5, 6, 7, 1, 3, 4, 10, 8, 9, 11, 14, 13, 15, 12):
        gather_one(0, peer).start()
    for step in (2, 1, 3):
        gather_one(2, step).start()

    small_copies[4].wait()

    def widen(g, carry):
        base = pl.multiple_of(g * (16 * FEAT), 128)
        strip = weight[:, pl.ds(base, 16 * FEAT)]
        gap = jnp.zeros((DN, 64 - FEAT), BF)
        for parity in range(2):
            for side in range(4):
                start = (parity * 4 + side) * FEAT
                wide[parity, side, :, pl.ds(pl.multiple_of(g * 128, 128), 128)] = jnp.concatenate(
                    [strip[:, start : start + FEAT], gap,
                     strip[:, start + 8 * FEAT : start + 9 * FEAT], gap], axis=1)
        return carry

    lax.fori_loop(0, 8, widen, 0)

    def weight_send(peer):
        turn, step = peer // 4, peer % 4
        return remote(
            wide.at[lax.rem(core + turn, 2), lax.rem(row_y + step, 4)], weights_all.at[peer],
            w_send.at[0], w_recv.at[0], column_peer(peer),
        )

    for peer in range(1, 8):
        weight_send(peer).start()
    weights_all[0] = wide[core, row_y]

    def to_second(k):
        arrived(gathered.at[0, k, pl.ds(1, 3)], g1_recv.at[k])
        for step in (2, 1, 3):
            gather_two(k, step).start()
        gather_three(k, 0, 4).start()

    def to_sibling(k):
        arrived(gathered.at[0, k, pl.ds(4, 12)], g2_recv.at[k])
        gather_three(k, 4, 12).start()

    def unpack(k, parity):
        for t in range(WIDE // 128):
            query_f32[k, t, parity * 256 : parity * 256 + 256] = (
                gathered[parity, k, :, :, 128 * t : 128 * t + 128].astype(F32).reshape(256, 128)
            )

    def arrive(k):
        unpack(k, 0)
        arrived(gathered.at[1, k], g3_recv.at[k])
        unpack(k, 1)

    to_second(1)
    arrived(gathered.at[0, 0, pl.ds(1, 7)], g1_recv.at[0])
    gather_three(0, 0, 8).start()
    arrived(gathered.at[0, 0, pl.ds(8, 8)], g1_recv.at[CHUNKS])
    gather_three(0, 8, 8).start()
    to_second(2)
    arrive(0)

    slots = lax.broadcasted_iota(jnp.int32, (1, SHARD), 1)

    def score(b, target):
        rows = []
        for s in range(S):
            r = b * S + s
            tiles = [
                query_f32[r // 16, t, pl.ds(r % 16, 32, stride=16), :] for t in range(WIDE // 128)
            ]
            rows.append(jnp.concatenate(tiles, axis=1)[:, :RANK])
        target[...] = dot(jnp.concatenate(rows, axis=0).astype(BF), cache[b], NN)

    def soften(b, source, target, stats):
        for s in range(S):
            last = lengths_ref[b] - S + s - kv * SHARD
            part = jnp.where(slots <= last, source[32 * s : 32 * s + 32, :], MASKED)
            top = jnp.max(part, axis=1, keepdims=True)
            weights = jnp.exp2((part - top) * FACTOR)
            total = jnp.sum(weights, axis=1, keepdims=True)
            target[32 * s : 32 * s + 32, :] = weights.astype(BF)
            stats[32 * s : 32 * s + 32, :] = stat_tile(top, total)

    def weigh(b, source, stats):
        numerators = dot(source[...], cache[b, :DC], NT)
        for s in range(S):
            r = b * S + s
            for t in range(DC // 128):
                partial[r // 16, t, pl.ds(r % 16, 32, stride=16), :] = numerators[
                    32 * s : 32 * s + 32, 128 * t : 128 * t + 128
                ]
            partial[r // 16, 4, pl.ds(r % 16, 32, stride=16), :] = stats[32 * s : 32 * s + 32, :]

    def pair_copy(k, start, count, channel):
        span = pl.ds(start, count)
        return remote(
            pair_send.at[k, span], pair_recv.at[k, span], pair_ss.at[k], pair_rs.at[channel], sibling
        )

    def first_copy(k, step):
        return remote(
            first_send.at[k, pl.ds(4 * step, 4)], first_recv.at[k, step - 1],
            r1_send.at[k], r1_recv.at[k], along_second(4 - step),
        )

    def second_copy(k, step):
        return remote(
            second_send.at[k, step], second_recv.at[k, step - 1],
            r2_send.at[k], r2_recv.at[k], along_first(4 - step),
        )

    def last_copy(peer):
        back = (4 - peer // 4) % 4 * 4 + (4 - peer % 4) % 4
        return remote(
            first_send.at[CHUNKS - 1, peer], last_recv.at[peer],
            r1_send.at[CHUNKS - 1], r1_recv.at[CHUNKS - 1], plane_peer(back),
        )

    def store_group(k, group, joined):
        tiles, top, total = joined
        tiles = tiles + [stat_tile(top, total)]
        for t in range(WIDE // 128):
            first_send[k, 4 * group : 4 * group + 4, :, 128 * t : 128 * t + 128] = (
                tiles[t].astype(BF).reshape(4, 16, 128)
            )

    def pack_pair(k, start, count):
        for t in range(WIDE // 128):
            pair_send[k, start : start + count, :, 128 * t : 128 * t + 128] = (
                partial[k, t, 256 + 16 * start : 256 + 16 * (start + count)]
                .astype(BF)
                .reshape(count, 16, 128)
            )

    def step_pair(k):
        pack_pair(k, 0, 16)
        pair_copy(k, 0, 16, k).start()

    def join_group(k, group):
        rows = slice(64 * group, 64 * group + 64)
        span = slice(4 * group, 4 * group + 4)
        own_part = (lambda t: partial[k, t, rows], partial[k, 4, rows])
        store_group(k, group, join([own_part, block_part(pair_recv, (k, span), 4)], spread))

    def step_first(k):
        arrived(pair_recv.at[k], pair_rs.at[k])
        for group in range(4):
            join_group(k, group)
        for step in (2, 1, 3):
            first_copy(k, step).start()

    def last_pair():
        for group in (2, 1, 3, 0):
            pack_pair(CHUNKS - 1, 4 * group, 4)
            pair_copy(CHUNKS - 1, 4 * group, 4, CHUNKS - 1 + group).start()

    def last_first():
        for group in (2, 1, 3, 0):
            arrived(pair_recv.at[CHUNKS - 1, pl.ds(4 * group, 4)], pair_rs.at[CHUNKS - 1 + group])
            join_group(CHUNKS - 1, group)
            for peer in range(max(1, 4 * group), 4 * group + 4):
                last_copy(peer).start()
        last_recv[0] = first_send[CHUNKS - 1, 0]

    def step_second(k):
        arrived(first_recv.at[k], r1_recv.at[k])
        parts = [block_part(first_send, (k, slice(0, 4)), 4)]
        parts += [block_part(first_recv, (k, step), 4) for step in range(3)]
        tiles, top, total = join(parts, spread)
        tiles = tiles + [stat_tile(top, total)]
        for t in range(WIDE // 128):
            second_send[k, :, :, 128 * t : 128 * t + 128] = tiles[t].astype(BF).reshape(4, 16, 128)
        for step in (2, 1, 3):
            second_copy(k, step).start()

    def step_last(k):
        if k < CHUNKS - 1:
            arrived(second_recv.at[k], r2_recv.at[k])
            parts = [block_part(second_send, (k, 0), 1)]
            parts += [block_part(second_recv, (k, step), 1) for step in range(3)]
            tiles, _, total = join(parts, spread)
        else:
            arrived(last_recv.at[pl.ds(1, 15)], r1_recv.at[k])
            tiles, _, total = join_stack(last_recv, spread)
        for t in range(DC // 128):
            latent[16 * k : 16 * k + 16, 128 * t : 128 * t + 128] = (tiles[t] / total).astype(BF)

    cache_copy(0).wait()
    score(0, scores_a)
    soften(0, scores_a, probs_a, stats_a)

    def after(b, schedule):
        for when, step, k in schedule:
            if b == when:
                step(k)

    def rollout_pair(i, carry):
        b = 2 * i
        cache_copy(i + 1).wait()
        score(b + 1, scores_b)
        weigh(b, probs_a, stats_a)
        soften(b + 1, scores_b, probs_b, stats_b)
        after(b, [(6, to_sibling, 2), (8, arrive, 2), (8, step_first, 0), (10, step_pair, 1), (12, step_first, 1)])
        score(b + 2, scores_a)
        weigh(b + 1, probs_b, stats_b)
        soften(b + 2, scores_a, probs_a, stats_a)
        after(b + 1, [(1, to_sibling, 1), (3, arrive, 1), (5, step_pair, 0)])
        return carry

    for i in range(B // 2 - 1):
        rollout_pair(i, 0)
    score(B - 1, scores_b)
    weigh(B - 2, probs_a, stats_a)
    soften(B - 1, scores_b, probs_b, stats_b)
    weigh(B - 1, probs_b, stats_b)
    last_pair()
    step_second(0)
    last_first()
    step_second(1)
    step_last(0)
    step_last(1)
    step_last(2)

    small_copies[5].wait()

    head_values = dot(latent[...], value_ref[...], NN).astype(BF)
    back = jnp.where(line == (column % S) * B + column // S, 1.0, 0.0).astype(BF)
    values[0] = dot(back, head_values, NN).astype(BF)

    def values_copy(peer):
        return remote(
            values.at[0], values.at[peer], v_send.at[0], v_recv.at[0], column_peer(peer)
        )

    for peer in range(1, 8):
        values_copy(peer).start()
    arrived(weights_all.at[pl.ds(1, 7)], w_recv.at[0])
    arrived(values.at[pl.ds(1, 7)], v_recv.at[0])

    all_values = jnp.concatenate([values[peer] for peer in range(8)], axis=1)
    def out_copy(over, beside):
        return remote(
            out_send.at[over, lax.rem(z + beside, 4)], out_recv.at[4 * over + beside - 1],
            o_send.at[0], o_recv.at[0], place(x + over, z + beside, core, row_y),
        )

    for over in (2, 1, 3, 0):
        lanes = pl.ds(pl.multiple_of(256 * lax.rem(x + over, 4), 256), 256)
        features = dot(all_values, weights_all[:, :, lanes].reshape(8 * DN, 256), NN)
        for slot in range(4):
            piece = features[:, 64 * slot : 64 * slot + 64]
            out_send[over, slot] = jnp.concatenate(
                [
                    jnp.concatenate([piece[:16], piece[16:32]], axis=1),
                    jnp.concatenate([piece[32:], jnp.zeros((16, 64), F32)], axis=1),
                ],
                axis=0,
            ).astype(BF)
        for beside in (2, 1, 3, 0):
            if over or beside:
                out_copy(over, beside).start()
    total = out_send[0, z].astype(F32)
    arrived(out_recv, o_recv.at[0])
    for peer in range(1, 16):
        total = total + out_recv[peer - 1].astype(F32)
    out_ref[...] = jnp.concatenate(
        [total[:16, :FEAT], total[:16, 64 : 64 + FEAT], total[16:, :FEAT]], axis=0
    ).astype(BF)

    for k in range(CHUNKS):
        departed(gathered.at[0, k, pl.ds(1, 15 if k == 0 else 3)], g1_send.at[k])
        departed(gathered.at[0, k], g3_send.at[k])
        departed(pair_recv.at[k], pair_ss.at[k])
        if k > 0:
            departed(gathered.at[0, k, pl.ds(4, 12)], g2_send.at[k])
        if k < CHUNKS - 1:
            departed(first_recv.at[k], r1_send.at[k])
            departed(second_recv.at[k], r2_send.at[k])
        else:
            departed(last_recv.at[pl.ds(1, 15)], r1_send.at[k])
    departed(weights_all.at[pl.ds(1, 7)], w_send.at[0])
    departed(values.at[pl.ds(1, 7)], v_send.at[0])
    departed(out_recv, o_send.at[0])


def body(query_heads, key_up, value_up, output_weight, latent_cache, lengths, positions):
    query = jnp.transpose(query_heads[:, :, 0, :], (1, 0, 2)).reshape(ROWS, DN + DR)
    cache = jnp.swapaxes(latent_cache, 1, 2)
    width = output_weight.shape[1]
    dma = pltpu.SemaphoreType.DMA
    vmem, smem = pltpu.VMEM, pltpu.SMEM
    out = pl.pallas_call(
        kernel,
        out_shape=jax.ShapeDtypeStruct((ROWS, FEAT), BF),
        in_specs=[
            pl.BlockSpec(memory_space=pl.ANY) for _ in range(7)
        ],
        out_specs=pl.BlockSpec(memory_space=vmem),
        scratch_shapes=[
            smem((B,), jnp.int32),
            smem((B,), jnp.int32),
            vmem((ROWS, DN + DR), BF),
            vmem((DN, DC), BF),
            vmem((DC, 128), BF),
            vmem((B, RANK, SHARD), BF),
            vmem((DN, width), BF),
            vmem((2, 4, DN, 1024), BF),
            vmem((8, DN, 1024), BF),
            vmem((2, CHUNKS, 16, 16, WIDE), BF),
            vmem((CHUNKS, WIDE // 128, 512, 128), F32),
            vmem((96, SHARD), F32),
            vmem((96, SHARD), F32),
            vmem((96, SHARD), BF),
            vmem((96, SHARD), BF),
            vmem((96, 128), F32),
            vmem((96, 128), F32),
            vmem((CHUNKS, WIDE // 128, 512, 128), F32),
            vmem((CHUNKS, 16, 16, WIDE), BF),
            vmem((CHUNKS, 16, 16, WIDE), BF),
            vmem((CHUNKS, 16, 16, WIDE), BF),
            vmem((CHUNKS, 3, 4, 16, WIDE), BF),
            vmem((CHUNKS, 4, 16, WIDE), BF),
            vmem((CHUNKS, 3, 16, WIDE), BF),
            vmem((ROWS, DC), BF),
            vmem((8, ROWS, 128), BF),
            vmem((4, 4, 32, 128), BF),
            vmem((15, 32, 128), BF),
            vmem((16, 16, WIDE), BF),
            vmem((128, 256), BF),
            dma((B // 2,)),
            dma((6,)),
            dma((CHUNKS,)), dma((CHUNKS + 1,)),
            dma((CHUNKS,)), dma((CHUNKS,)),
            dma((CHUNKS,)), dma((CHUNKS,)),
            dma((CHUNKS,)), dma((CHUNKS + 3,)),
            dma((CHUNKS,)), dma((CHUNKS,)),
            dma((CHUNKS,)), dma((CHUNKS,)),
            dma((1,)), dma((1,)),
            dma((1,)), dma((1,)),
            dma((1,)), dma((1,)),
        ],
        compiler_params=pltpu.CompilerParams(
            collective_id=0, has_side_effects=True, vmem_limit_bytes=56 * 2**20
        ),
    )(lengths, positions, query, key_up[0], value_up[0], output_weight, cache)
    return jnp.transpose(out.reshape(S, B, FEAT), (1, 0, 2))


def solution(mesh):
    in_specs = (
        P(None, None, ("kv", "head"), None),
        P(("kv", "head"), None, None),
        P(("kv", "head"), None, None),
        P(("kv", "head"), None),
        P(None, "kv", None),
        P(),
        P(),
    )
    out_specs = P(None, None, ("kv", "head"))
    return jax.shard_map(body, mesh=mesh, in_specs=in_specs, out_specs=out_specs, check_vma=False)
```
